512 devices in a mesh: row: 32 (over z, core), col: 16 (over x, y).
Axes of the slice: x: 4, y: 4, z: 16, core: 2. Of those that a mesh axis runs over, the one named last changes fastest.
Arguments:
- covariance: float32 [8192, 8192], P('row', 'col'), as said below
- state_mean: float32 [8192], P('row'), may hold values from -6 to 6
- obs_values: float32 [2, 256], replicated, may hold values from -8 to 8
- obs_cells: int32 [2, 4, 256], replicated, may hold values from 0 to 8191
- obs_weights: float32 [2, 4, 256], replicated, may hold values from 0.2 to 1
- obs_variance: float32 [2, 256], replicated, may hold values from 0.05 to 1
Outputs:
- covariance_after: float32 [8192, 8192], P('row', 'col')
- state_after: float32 [8192], P('row')
The draws below stay inside these ranges and needn't reach their ends.
Inputs may be any that keep to these rules, and one draw needn't show every extreme that they name: `covariance`: symmetric and positive definite.
All inputs are finite; a program needn't handle non-finite values.
Results may differ from the reference program's by a relative error of at most 0.0001.
Values sent between devices are 32-bit elements; how exact they have to be, the bound alone decides.
No kernel may reach another device: no remote copies, remote signals or barrier semaphores. Data moves between devices by JAX's collectives and lax.ppermute only.
A program may use at most 64 MiB of HBM per device.

```python
import math
import jax
import jax.numpy as jnp
from jax import lax

STATE = 8192
OBS = 256
FOOT = 4
BATCHES = 2


def draw_covariance(key, part):
    noise = jax.random.normal(jax.random.fold_in(key, 11), (STATE, STATE), jnp.float32)
    sym = (noise + noise.T) * (0.35 / math.sqrt(STATE))
    diag = jax.random.uniform(jax.random.fold_in(key, 12), (STATE,), jnp.float32, 1.5, 2.5)
    matrix = sym + jnp.diag(diag)
    return matrix


def place_ends(drawn, own_key, least, high):
    shape = drawn.shape
    spot = [jax.random.randint(jax.random.fold_in(own_key, axis), (), 0, shape[axis]) for axis in range(len(shape))]
    drawn = drawn.at[tuple(spot)].set(least)
    longest = shape.index(max(shape))
    spot[longest] = (spot[longest] + 1) % shape[longest]
    return drawn.at[tuple(spot)].set(high)


def block_levels(key, shape, split, smallest, top_value):
    level, own = 1.0, jax.random.fold_in(key, 6)
    for position, blocks in split:
        steps = jnp.exp(jax.random.uniform(jax.random.fold_in(own, position), (blocks,), jnp.float32, smallest / len(split), top_value / len(split)))
        level = level * jnp.repeat(steps, shape[position] // blocks).reshape([-1 if axis == position else 1 for axis in range(len(shape))])
    return level


def bell_draw(rng, shape, scale, limit, shards=(), kind=jnp.bfloat16):
    array = jax.random.normal(rng, shape, jnp.float32) * scale
    if len(shards) > 0:
        array = block_levels(rng, shape, shards, -0.22, 0.18) * array
    return jnp.clip(array, min=-limit, max=limit).astype(kind)


def setup_inputs(seed: int = 0) -> dict:
    seeds = jax.random.split(jax.random.key(seed), 7)
    covariance = draw_covariance(jax.random.fold_in(seeds[6], 71), 0)
    state_mean = bell_draw(seeds[1], (STATE,), 1.0, 6.0, ((0, 32),), jnp.float32)
    obs_values = bell_draw(seeds[2], (BATCHES, OBS), 2.0, 8.0, (), jnp.float32)
    obs_cells = place_ends(jax.random.randint(seeds[3], (BATCHES, FOOT, OBS), 0, STATE), jax.random.fold_in(seeds[3], 1), 0, STATE - 1).astype(jnp.int32)
    obs_weights = jnp.clip(jax.random.uniform(seeds[4], (BATCHES, FOOT, OBS), jnp.float32, 0.2, 1.0), 0.2, 1.0)
    obs_variance = jnp.clip(jnp.exp(jax.random.uniform(seeds[5], (BATCHES, OBS), jnp.float32, math.log(0.05), math.log(1.0))), 0.05, 1.0)
    return {"covariance": covariance, "state_mean": state_mean, "obs_values": obs_values, "obs_cells": obs_cells, "obs_weights": obs_weights, "obs_variance": obs_variance}


def reference(covariance, state_mean, obs_values, obs_cells, obs_weights, obs_variance):
    hi = lax.Precision.HIGHEST
    matrix = covariance
    mean = state_mean
    for batch in range(BATCHES):
        cells = obs_cells[batch]
        weights = obs_weights[batch]
        cross = jnp.zeros((STATE, OBS), jnp.float32)
        for foot in range(FOOT):
            cross = cross + matrix[:, cells[foot]] * weights[foot][None, :]
        inner = jnp.zeros((OBS, OBS), jnp.float32)
        predicted = jnp.zeros((OBS,), jnp.float32)
        for foot in range(FOOT):
            inner = inner + weights[foot][:, None] * cross[cells[foot], :]
            predicted = predicted + weights[foot] * mean[cells[foot]]
        inner = 0.5 * (inner + inner.T) + jnp.diag(obs_variance[batch])
        factor = jnp.linalg.cholesky(inner)
        gain = lax.linalg.triangular_solve(factor, cross.T, left_side=True, lower=True).T
        innov = (obs_values[batch] - predicted)[:, None]
        white = lax.linalg.triangular_solve(factor, innov, left_side=True, lower=True)[:, 0]
        mean = mean + jnp.dot(gain.astype(jnp.float32), white.astype(jnp.float32), precision=hi, preferred_element_type=jnp.float32)
        matrix = matrix - jnp.dot(gain.astype(jnp.float32), gain.T.astype(jnp.float32), precision=hi, preferred_element_type=jnp.float32)
    return (matrix, mean)
```

```python
import jax
import jax.numpy as jnp
from jax import lax
from jax.sharding import PartitionSpec as P

LANES = 128
HI = lax.Precision.HIGHEST


def dot(a, b):
    return jnp.dot(a, b, precision=HI, preferred_element_type=jnp.float32)


def local_operator(cells, weights, start, count):
    positions = start + lax.iota(jnp.int32, count)[:, None]
    total = jnp.zeros((count, cells.shape[1]), jnp.float32)
    for foot in range(cells.shape[0]):
        total = total + jnp.where(cells[foot][None, :] == positions, weights[foot][None, :], 0.0)
    return total


def lower_blocks(n):
    return [(i, j) for i in range(n) for j in range(i + 1)]


def on_device(covariance, state_mean, obs_values, obs_cells, obs_weights, obs_variance):
    rows, cols = covariance.shape
    n_row, n_col = lax.axis_size("row"), lax.axis_size("col")
    n_z = n_row // 2
    row, col = lax.axis_index("row"), lax.axis_index("col")
    core = lax.rem(row, 2)
    plane = 2 * n_col
    batches, foot, obs = obs_cells.shape
    m = batches * obs
    nb = m // LANES
    cells = obs_cells.transpose(1, 0, 2).reshape(foot, m)
    weights = obs_weights.transpose(1, 0, 2).reshape(foot, m)
    values = obs_values.reshape(m)
    variance = obs_variance.reshape(m)

    plane_groups = [[z * plane + i for i in range(plane)] for z in range(n_z)]
    z_groups = [[2 * z + k for z in range(n_z)] for k in range(2)]

    col_op = local_operator(cells, weights, col * cols, cols)
    row_op = local_operator(cells, weights, row * rows, rows)
    c_part = dot(covariance, col_op)
    s_part = dot(row_op.T, c_part)
    pred = jnp.where(col == 0, dot(state_mean[None, :], row_op)[0], 0.0)

    low = lower_blocks(nb)
    blocks = []
    r_io = lax.broadcasted_iota(jnp.int32, (LANES, LANES), 0)
    l_io = lax.broadcasted_iota(jnp.int32, (LANES, LANES), 1)
    for i, j in low:
        blk = s_part[i * LANES:(i + 1) * LANES, j * LANES:(j + 1) * LANES]
        if i == j:
            p = pred[i * LANES:(i + 1) * LANES]
            blk = jnp.where((r_io == 0) & (l_io > 0), p[None, :], blk)
            blk = jnp.where((r_io == 1) & (l_io == LANES - 1), p[0], blk)
        blocks.append(blk)
    s_rows = len(low) * LANES // plane
    s_send = jnp.concatenate(blocks, axis=0).reshape(plane, s_rows, LANES)
    own = rows // plane
    c_rows = own * nb
    c_send = c_part.reshape(plane, own, nb, LANES).transpose(0, 2, 1, 3).reshape(plane, c_rows, LANES)
    send = jnp.concatenate([s_send, c_send], axis=1)
    got = lax.all_to_all(send, ("row", "col"), 0, 0, axis_index_groups=plane_groups)
    s_chunk = jnp.sum(got[:, :s_rows], axis=0)
    c_own = jnp.sum(got[:, s_rows:].reshape(2, n_col, c_rows, LANES), axis=1)

    total = n_row * n_col
    pairs = []
    for idx in range(total):
        rr, cc = divmod(idx, n_col)
        z, k = divmod(rr, 2)
        pairs.append((idx, (2 * cc + k) * n_col + z))
    c_tr = lax.ppermute(c_own, ("row", "col"), pairs)

    s_all = lax.all_to_all(
        jnp.broadcast_to(s_chunk[None], (n_z, s_rows, LANES)), "row", 0, 0, axis_index_groups=z_groups
    )
    s_full = jnp.sum(s_all, axis=0)

    send2 = jnp.concatenate(
        [
            jnp.broadcast_to(s_full[None], (plane, s_rows, LANES)),
            jnp.broadcast_to(c_own[:, None], (2, n_col, c_rows, LANES)).reshape(plane, c_rows, LANES),
        ],
        axis=1,
    )
    got2 = lax.all_to_all(send2, ("row", "col"), 0, 0, axis_index_groups=plane_groups)
    flat = got2[:, :s_rows].reshape(len(low), LANES, LANES)
    c_r = got2[:, s_rows:].reshape(plane, nb, own, LANES).transpose(0, 2, 1, 3).reshape(rows, m)

    c_z = lax.all_to_all(
        jnp.broadcast_to(c_tr[None], (n_z,) + c_tr.shape), "row", 0, 0, axis_index_groups=z_groups
    )
    c_other = lax.ppermute(c_z, "row", [(i, i ^ 1) for i in range(n_row)])
    first = jnp.where(core == 0, c_z, c_other)
    second = jnp.where(core == 0, c_other, c_z)
    both = jnp.stack([first, second], axis=0)
    c_c = both.reshape(2, n_z, 2, nb, own, LANES).transpose(2, 0, 1, 4, 3, 5).reshape(2 * rows, m)

    grid = [[None] * nb for _ in range(nb)]
    predicted = []
    for b, (i, j) in enumerate(low):
        blk = flat[b]
        if i == j:
            predicted.append(jnp.where(jnp.arange(LANES) == 0, blk[1, LANES - 1], blk[0]))
            tri = jnp.tril(blk)
            blk = tri + jnp.tril(blk, -1).T
            grid[i][i] = blk
        else:
            grid[i][j] = blk
            grid[j][i] = blk.T
    inner = jnp.concatenate([jnp.concatenate(g, axis=1) for g in grid], axis=0) + jnp.diag(variance)
    factor = jnp.linalg.cholesky(inner)
    inv = lax.linalg.triangular_solve(factor, jnp.eye(m, dtype=jnp.float32), left_side=True, lower=True)
    white = dot(inv, (values - jnp.concatenate(predicted))[:, None])[:, 0]
    g_r = dot(c_r, inv.T)
    g_c = dot(c_c, inv.T)
    mean = state_mean + dot(g_r, white[:, None])[:, 0]
    return (covariance - dot(g_r, g_c.T), mean)


def solution(mesh):
    return jax.shard_map(
        on_device,
        mesh=mesh,
        in_specs=(P("row", "col"), P("row"), P(), P(), P(), P()),
        out_specs=(P("row", "col"), P("row")),
        check_vma=False,
    )
```

```python
import jax
import jax.numpy as jnp
from jax import lax
from jax.experimental import pallas as pl
from jax.experimental.pallas import tpu as pltpu
from jax.sharding import PartitionSpec as P

SUB = 8
LANES = 128
GROUPS = LANES // SUB
HI = lax.Precision.HIGHEST
VMEM = pl.BlockSpec(memory_space=pltpu.VMEM)
SMEM = pl.BlockSpec(memory_space=pltpu.SMEM)
LIMIT = 48 * 1024 * 1024


def dot(a, b):
    return jnp.dot(a, b, precision=HI, preferred_element_type=jnp.float32)


def dot_dims(a, b, da, db):
    return lax.dot_general(
        a, b, (((da,), (db,)), ((), ())), precision=HI, preferred_element_type=jnp.float32
    )


def wide(x):
    return jnp.broadcast_to(x, (SUB, LANES))


def lower_blocks(n):
    return [(i, j) for i in range(n) for j in range(i + 1)]


def call(kernel, out_shape, specs, scratch=(), flops=0, name=None):
    return pl.pallas_call(
        kernel,
        out_shape=out_shape,
        in_specs=specs,
        out_specs=jax.tree.map(lambda _: VMEM, out_shape),
        scratch_shapes=list(scratch),
        compiler_params=pltpu.CompilerParams(vmem_limit_bytes=LIMIT),
        cost_estimate=pl.CostEstimate(flops=flops, bytes_accessed=1 << 20, transcendentals=0),
        name=name,
    )


def shape(*dims):
    return jax.ShapeDtypeStruct(dims, jnp.float32)


def operator(cells_ref, weights_ref, batch, start, count):
    foot, obs = cells_ref.shape[1], cells_ref.shape[2]
    positions = start + lax.broadcasted_iota(jnp.int32, (count, obs), 0)
    total = jnp.zeros((count, obs), jnp.float32)
    for f in range(foot):
        hit = cells_ref[batch, f:f + 1, :] == positions
        total = total + jnp.where(hit, weights_ref[batch, f:f + 1, :], 0.0)
    return total


def project_kernel(at_ref, cov_ref, mean_ref, cells_ref, weights_ref, send_ref, c_ref, s_ref):
    rows, cols = cov_ref.shape
    batches, _, obs = cells_ref.shape
    plane = send_ref.shape[0]
    nb = batches * obs // LANES
    per = obs // LANES
    row_ops = []
    cov = cov_ref[...]
    for b in range(batches):
        col_op = operator(cells_ref, weights_ref, b, at_ref[1] * cols, cols)
        row_ops.append(operator(cells_ref, weights_ref, b, at_ref[0] * rows, rows))
        c_ref[:, b * obs:(b + 1) * obs] = dot(cov, col_op)
    for i in range(batches):
        for j in range(i + 1):
            s_ref[i * obs:(i + 1) * obs, j * obs:(j + 1) * obs] = dot_dims(
                row_ops[i], c_ref[:, j * obs:(j + 1) * obs], 0, 0
            )
    low = lower_blocks(nb)
    tiles = len(low) * GROUPS // plane
    lane = lax.broadcasted_iota(jnp.int32, (SUB, LANES), 1)
    sub = lax.broadcasted_iota(jnp.int32, (SUB, LANES), 0)
    mean = jnp.broadcast_to(mean_ref[...], (SUB, rows))
    mean = jnp.where(at_ref[1] == 0, mean, 0.0)
    preds = [dot(mean, row_ops[b]) for b in range(batches)]
    for n, (i, j) in enumerate(low):
        for g in range(GROUPS):
            t = s_ref[i * LANES + g * SUB:i * LANES + (g + 1) * SUB, j * LANES:(j + 1) * LANES]
            if i == j and g == 0:
                p = preds[i // per][:, (i % per) * LANES:(i % per + 1) * LANES]
                t = jnp.where((sub == 0) & (lane > 0), p, t)
                t = jnp.where((sub == 1) & (lane == LANES - 1), wide(p[:, :1]), t)
            q = n * GROUPS + g
            send_ref[q // tiles, (q % tiles) * SUB:(q % tiles + 1) * SUB, :] = t
    own = rows // plane
    for i in range(plane):
        for j in range(nb):
            at = (tiles + j) * SUB
            send_ref[i, at:at + own, :] = c_ref[i * own:(i + 1) * own, j * LANES:(j + 1) * LANES]


def inverse_factor(v):
    v = list(v)
    lane = lax.broadcasted_iota(jnp.int32, (SUB, LANES), 1)
    sub = lax.broadcasted_iota(jnp.int32, (SUB, LANES), 0)
    odd = (sub % 2) == 1

    def swap(z):
        return jnp.where(odd, pltpu.roll(z, 1, 0), pltpu.roll(z, SUB - 1, 0))

    out = []
    for p in range(len(v)):
        t = v[p]
        base = p * SUB
        inside = (lane >= base) & (lane < base + SUB)
        col = [wide(t[:, base + s:base + s + 1]) for s in range(SUB)]
        t = jnp.where(inside, jnp.where(lane - base == sub, 1.0, 0.0), t)
        low = t
        same = cross = step = jnp.zeros((SUB, LANES), jnp.float32)
        piv = jnp.ones((SUB, LANES), jnp.float32)
        for u in range(0, SUB, 2):
            a = wide(col[u][u:u + 1])
            b = wide(col[u + 1][u:u + 1])
            c = wide(col[u + 1][u + 1:u + 2])
            det = a * c - b * b
            rd = pltpu.reciprocal(det, approx=True)
            ra = pltpu.reciprocal(a, approx=True)
            here = (sub == u) | (sub == u + 1)
            c1 = jnp.where(here, 0.0, col[u])
            c2 = jnp.where(here, 0.0, col[u + 1])
            m1 = (c1 * c - c2 * b) * rd
            m2 = (c2 * a - c1 * b) * rd
            for w in range(u + 2, SUB):
                col[w] = col[w] - (m1 * wide(col[w][u:u + 1]) + m2 * wide(col[w][u + 1:u + 2]))
            t = t - (m1 * wide(t[u:u + 1]) + m2 * wide(t[u + 1:u + 2]))
            low = low - jnp.where(
                sub > u + 1, m1 * wide(low[u:u + 1]) + m2 * wide(low[u + 1:u + 2]), 0.0
            )
            same = jnp.where(sub == u, c * rd, jnp.where(sub == u + 1, a * rd, same))
            cross = jnp.where(here, b * rd, cross)
            step = jnp.where(sub == u + 1, b * ra, step)
            piv = jnp.where(sub == u, a, jnp.where(sub == u + 1, det * ra, piv))
        q = t * same - swap(t) * cross
        x = (low - step * swap(low)) * lax.rsqrt(piv)
        out.append(jnp.where(lane <= sub + base, x, 0.0))
        for j in range(p + 1, len(v)):
            w = v[j]
            c = [wide(w[:, base + s:base + s + 1]) * wide(q[s:s + 1]) for s in range(SUB)]
            w = jnp.where(inside, 0.0, w)
            v[j] = w - (((c[0] + c[1]) + (c[2] + c[3])) + ((c[4] + c[5]) + (c[6] + c[7])))
    return out


def factor_kernel(got_ref, values_ref, variance_ref, linv_ref, white_ref, a_ref, l_ref):
    nb = values_ref.shape[0]
    low = lower_blocks(nb)
    plane = got_ref.shape[0]
    tiles = len(low) * GROUPS // plane
    for n, (i, j) in enumerate(low):
        for g in range(GROUPS):
            q = n * GROUPS + g
            a_ref[i, j, g * SUB:(g + 1) * SUB, :] = got_ref[
                q // tiles, (q % tiles) * SUB:(q % tiles + 1) * SUB, :
            ]
    r_io = lax.broadcasted_iota(jnp.int32, (LANES, LANES), 0)
    l_io = lax.broadcasted_iota(jnp.int32, (LANES, LANES), 1)
    lane = lax.broadcasted_iota(jnp.int32, (SUB, LANES), 1)
    innov = []
    for i in range(nb):
        first = a_ref[i, i, 0:SUB, :]
        pred = jnp.where(lane == 0, wide(first[1:2, LANES - 1:LANES]), wide(first[0:1, :]))
        innov.append(wide(values_ref[i:i + 1, :]) - pred)
        d = a_ref[i, i]
        below = jnp.where(r_io > l_io, d, 0.0)
        diag = jnp.where(r_io == l_io, d + variance_ref[i:i + 1, :], 0.0)
        a_ref[i, i] = below + below.T + diag
    for i in range(nb):
        for j in range(i + 1, nb):
            linv_ref[i * LANES:(i + 1) * LANES, j * LANES:(j + 1) * LANES] = jnp.zeros(
                (LANES, LANES), jnp.float32
            )
    for i in range(nb):
        x = jnp.concatenate(
            inverse_factor([a_ref[i, i, g * SUB:(g + 1) * SUB, :] for g in range(GROUPS)]), axis=0
        )
        at = slice(i * LANES, (i + 1) * LANES)
        for j in range(i + 1, nb):
            l_ref[j, i] = dot_dims(a_ref[j, i], x, 1, 1)
        for k in range(i + 1, nb):
            for j in range(k, nb):
                a_ref[j, k] = a_ref[j, k] - dot_dims(l_ref[j, i], l_ref[k, i], 1, 1)
        linv_ref[at, at] = x
        if i > 0:
            acc = dot(l_ref[i, 0], linv_ref[0:LANES, 0:i * LANES])
            for k in range(1, i):
                acc = acc + dot(l_ref[i, k], linv_ref[k * LANES:(k + 1) * LANES, 0:i * LANES])
            linv_ref[at, 0:i * LANES] = -dot(x, acc)
    white_ref[...] = dot_dims(jnp.concatenate(innov, axis=1), linv_ref[...], 1, 1)


def rows_kernel(got_ref, linv_ref, white_ref, mean_ref, gain_ref, after_ref, c_ref):
    plane = got_ref.shape[0]
    rows, m = gain_ref.shape
    own = rows // plane
    nb = m // LANES
    skip = got_ref.shape[1] - nb * own
    for i in range(plane):
        for j in range(nb):
            at = skip + j * own
            c_ref[i * own:(i + 1) * own, j * LANES:(j + 1) * LANES] = got_ref[i, at:at + own, :]
    gain = dot_dims(c_ref[...], linv_ref[...], 1, 1)
    gain_ref[...] = gain
    after_ref[...] = dot_dims(white_ref[...], gain, 1, 1) + mean_ref[...]


def update_kernel(at_ref, cov_ref, mine_ref, other_ref, linv_ref, gain_ref, out_ref, c_ref):
    n_z, halves, tall, _ = mine_ref.shape
    cols, m = c_ref.shape
    nb = m // LANES
    own = tall // nb
    core = at_ref[2]
    for ref, k in ((mine_ref, core), (other_ref, 1 - core)):
        start = pl.multiple_of(k * (n_z * own), n_z * own)
        for h in range(halves):
            for z in range(n_z):
                for j in range(nb):
                    at = h * (cols // halves) + z * own
                    c_ref[pl.ds(start + at, own), j * LANES:(j + 1) * LANES] = ref[
                        z, h, j * own:(j + 1) * own, :
                    ]
    gain_cols = dot_dims(c_ref[...], linv_ref[...], 1, 1)
    out_ref[...] = cov_ref[...] - dot_dims(gain_ref[...], gain_cols, 1, 1)


def on_device(covariance, state_mean, obs_values, obs_cells, obs_weights, obs_variance):
    rows, cols = covariance.shape
    n_row, n_col = lax.axis_size("row"), lax.axis_size("col")
    n_z = n_row // 2
    row, col = lax.axis_index("row"), lax.axis_index("col")
    core = lax.rem(row, 2)
    plane = 2 * n_col
    batches, _, obs = obs_cells.shape
    m = batches * obs
    nb = m // LANES
    own = rows // plane
    c_rows = own * nb
    s_rows = nb * (nb + 1) // 2 * LANES // plane
    chunk = s_rows + c_rows
    at = jnp.stack([row, col, core]).astype(jnp.int32)
    mean = state_mean.reshape(1, rows)

    plane_groups = [[z * plane + i for i in range(plane)] for z in range(n_z)]
    z_groups = [[2 * z + k for z in range(n_z)] for k in range(2)]
    pairs = []
    for idx in range(n_row * n_col):
        r, c = divmod(idx, n_col)
        z, k = divmod(r, 2)
        pairs.append((idx, (2 * c + k) * n_col + z))

    send = call(
        project_kernel,
        shape(plane, chunk, LANES),
        [SMEM, VMEM, VMEM, VMEM, VMEM],
        [pltpu.VMEM((rows, m), jnp.float32), pltpu.VMEM((m, m), jnp.float32)],
        flops=2 * rows * m * (cols + m),
        name="project",
    )(at, covariance, mean, obs_cells, obs_weights)
    got = lax.all_to_all(send, ("row", "col"), 0, 0, axis_index_groups=plane_groups)
    s_chunk = jnp.sum(got[:, :s_rows], axis=0)
    c_own = jnp.sum(got[:, s_rows:].reshape(2, n_col, c_rows, LANES), axis=1)

    c_tr = lax.ppermute(c_own, ("row", "col"), pairs)
    s_all = lax.all_to_all(
        jnp.broadcast_to(s_chunk[None], (n_z, s_rows, LANES)), "row", 0, 0, axis_index_groups=z_groups
    )
    s_full = jnp.sum(s_all, axis=0)
    send2 = jnp.concatenate(
        [
            jnp.broadcast_to(s_full[None], (plane, s_rows, LANES)),
            jnp.broadcast_to(c_own[:, None], (2, n_col, c_rows, LANES)).reshape(plane, c_rows, LANES),
        ],
        axis=1,
    )
    got2 = lax.all_to_all(send2, ("row", "col"), 0, 0, axis_index_groups=plane_groups)

    c_tr, got2 = lax.optimization_barrier((c_tr, got2))
    c_z = lax.all_to_all(
        jnp.broadcast_to(c_tr[None], (n_z,) + c_tr.shape), "row", 0, 0, axis_index_groups=z_groups
    )
    linv, white = call(
        factor_kernel,
        (shape(m, m), shape(SUB, m)),
        [VMEM] * 3,
        [pltpu.VMEM((nb, nb, LANES, LANES), jnp.float32), pltpu.VMEM((nb, nb, LANES, LANES), jnp.float32)],
        flops=1 << 34,
        name="factor",
    )(got2, obs_values.reshape(nb, LANES), obs_variance.reshape(nb, LANES))
    c_other = lax.ppermute(c_z, "row", [(i, i ^ 1) for i in range(n_row)])
    gain, after = call(
        rows_kernel,
        (shape(rows, m), shape(SUB, rows)),
        [VMEM] * 4,
        [pltpu.VMEM((rows, m), jnp.float32)],
        flops=1 << 31,
        name="rows",
    )(got2, linv, white, mean)
    updated = call(
        update_kernel,
        shape(rows, cols),
        [SMEM] + [VMEM] * 5,
        [pltpu.VMEM((cols, m), jnp.float32)],
        flops=1 << 31,
        name="update",
    )(at, covariance, c_z, c_other, linv, gain)
    return (updated, after[0])


def solution(mesh):
    return jax.shard_map(
        on_device,
        mesh=mesh,
        in_specs=(P("row", "col"), P("row"), P(), P(), P(), P()),
        out_specs=(P("row", "col"), P("row")),
        check_vma=False,
    )
```

```python
import jax
import jax.numpy as jnp
from jax import lax
from jax.experimental import pallas as pl
from jax.experimental.pallas import tpu as pltpu
from jax.sharding import PartitionSpec as P

SUB = 8
LANES = 128
GROUPS = LANES // SUB
HI = lax.Precision.HIGHEST
VMEM = pl.BlockSpec(memory_space=pltpu.VMEM)
SMEM = pl.BlockSpec(memory_space=pltpu.SMEM)
LIMIT = 48 * 1024 * 1024


def dot(a, b):
    return jnp.dot(a, b, precision=HI, preferred_element_type=jnp.float32)


def dot_dims(a, b, da, db):
    return lax.dot_general(
        a, b, (((da,), (db,)), ((), ())), precision=HI, preferred_element_type=jnp.float32
    )


def wide(x):
    return jnp.broadcast_to(x, (SUB, LANES))


def lower_blocks(n):
    return [(i, j) for i in range(n) for j in range(i + 1)]


def call(kernel, out_shape, specs, scratch=(), flops=0, name=None):
    return pl.pallas_call(
        kernel,
        out_shape=out_shape,
        in_specs=specs,
        out_specs=jax.tree.map(lambda _: VMEM, out_shape),
        scratch_shapes=list(scratch),
        compiler_params=pltpu.CompilerParams(vmem_limit_bytes=LIMIT),
        cost_estimate=pl.CostEstimate(flops=flops, bytes_accessed=1 << 20, transcendentals=0),
        name=name,
    )


def shape(*dims):
    return jax.ShapeDtypeStruct(dims, jnp.float32)


def operator(cells_ref, weights_ref, batch, start, count):
    foot, obs = cells_ref.shape[1], cells_ref.shape[2]
    positions = start + lax.broadcasted_iota(jnp.int32, (count, obs), 0)
    total = jnp.zeros((count, obs), jnp.float32)
    for f in range(foot):
        hit = cells_ref[batch, f:f + 1, :] == positions
        total = total + jnp.where(hit, weights_ref[batch, f:f + 1, :], 0.0)
    return total


def project_kernel(at_ref, cov_ref, mean_ref, cells_ref, weights_ref, send_ref, c_ref, s_ref):
    rows, cols = cov_ref.shape
    batches, _, obs = cells_ref.shape
    plane = send_ref.shape[0]
    nb = batches * obs // LANES
    per = obs // LANES
    row_ops = []
    cov = cov_ref[...]
    for b in range(batches):
        col_op = operator(cells_ref, weights_ref, b, at_ref[1] * cols, cols)
        row_ops.append(operator(cells_ref, weights_ref, b, at_ref[0] * rows, rows))
        c_ref[:, b * obs:(b + 1) * obs] = dot(cov, col_op)
    for i in range(batches):
        for j in range(i + 1):
            s_ref[i * obs:(i + 1) * obs, j * obs:(j + 1) * obs] = dot_dims(
                row_ops[i], c_ref[:, j * obs:(j + 1) * obs], 0, 0
            )
    low = lower_blocks(nb)
    tiles = len(low) * GROUPS // plane
    lane = lax.broadcasted_iota(jnp.int32, (SUB, LANES), 1)
    sub = lax.broadcasted_iota(jnp.int32, (SUB, LANES), 0)
    mean = jnp.broadcast_to(mean_ref[...], (SUB, rows))
    mean = jnp.where(at_ref[1] == 0, mean, 0.0)
    preds = [dot(mean, row_ops[b]) for b in range(batches)]
    for n, (i, j) in enumerate(low):
        for g in range(GROUPS):
            t = s_ref[i * LANES + g * SUB:i * LANES + (g + 1) * SUB, j * LANES:(j + 1) * LANES]
            if i == j and g == 0:
                p = preds[i // per][:, (i % per) * LANES:(i % per + 1) * LANES]
                t = jnp.where((sub == 0) & (lane > 0), p, t)
                t = jnp.where((sub == 1) & (lane == LANES - 1), wide(p[:, :1]), t)
            q = n * GROUPS + g
            send_ref[q // tiles, (q % tiles) * SUB:(q % tiles + 1) * SUB, :] = t
    own = rows // plane
    for i in range(plane):
        for j in range(nb):
            at = (tiles + j) * SUB
            send_ref[i, at:at + own, :] = c_ref[i * own:(i + 1) * own, j * LANES:(j + 1) * LANES]


def inverse_factor(v):
    v = list(v)
    lane = lax.broadcasted_iota(jnp.int32, (SUB, LANES), 1)
    sub = lax.broadcasted_iota(jnp.int32, (SUB, LANES), 0)
    odd = (sub % 2) == 1

    def swap(z):
        return jnp.where(odd, pltpu.roll(z, 1, 0), pltpu.roll(z, SUB - 1, 0))

    out = []
    for p in range(len(v)):
        t = v[p]
        base = p * SUB
        inside = (lane >= base) & (lane < base + SUB)
        col = [wide(t[:, base + s:base + s + 1]) for s in range(SUB)]
        t = jnp.where(inside, jnp.where(lane - base == sub, 1.0, 0.0), t)
        low = t
        same = cross = step = jnp.zeros((SUB, LANES), jnp.float32)
        piv = jnp.ones((SUB, LANES), jnp.float32)
        for u in range(0, SUB, 2):
            a = wide(col[u][u:u + 1])
            b = wide(col[u + 1][u:u + 1])
            c = wide(col[u + 1][u + 1:u + 2])
            det = a * c - b * b
            rd = pltpu.reciprocal(det, approx=True)
            ra = pltpu.reciprocal(a, approx=True)
            here = (sub == u) | (sub == u + 1)
            c1 = jnp.where(here, 0.0, col[u])
            c2 = jnp.where(here, 0.0, col[u + 1])
            m1 = (c1 * c - c2 * b) * rd
            m2 = (c2 * a - c1 * b) * rd
            for w in range(u + 2, SUB):
                col[w] = col[w] - (m1 * wide(col[w][u:u + 1]) + m2 * wide(col[w][u + 1:u + 2]))
            t = t - (m1 * wide(t[u:u + 1]) + m2 * wide(t[u + 1:u + 2]))
            low = low - jnp.where(
                sub > u + 1, m1 * wide(low[u:u + 1]) + m2 * wide(low[u + 1:u + 2]), 0.0
            )
            same = jnp.where(sub == u, c * rd, jnp.where(sub == u + 1, a * rd, same))
            cross = jnp.where(here, b * rd, cross)
            step = jnp.where(sub == u + 1, b * ra, step)
            piv = jnp.where(sub == u, a, jnp.where(sub == u + 1, det * ra, piv))
        q = t * same - swap(t) * cross
        x = (low - step * swap(low)) * lax.rsqrt(piv)
        out.append(jnp.where(lane <= sub + base, x, 0.0))
        for j in range(p + 1, len(v)):
            w = v[j]
            c = [wide(w[:, base + s:base + s + 1]) * wide(q[s:s + 1]) for s in range(SUB)]
            w = jnp.where(inside, 0.0, w)
            v[j] = w - (((c[0] + c[1]) + (c[2] + c[3])) + ((c[4] + c[5]) + (c[6] + c[7])))
    return out


def factor_kernel(got_ref, values_ref, variance_ref, linv_ref, white_ref, a_ref, l_ref):
    nb = values_ref.shape[0]
    low = lower_blocks(nb)
    plane = got_ref.shape[0]
    tiles = len(low) * GROUPS // plane
    for n, (i, j) in enumerate(low):
        for g in range(GROUPS):
            q = n * GROUPS + g
            a_ref[i, j, g * SUB:(g + 1) * SUB, :] = got_ref[
                q // tiles, (q % tiles) * SUB:(q % tiles + 1) * SUB, :
            ]
    r_io = lax.broadcasted_iota(jnp.int32, (LANES, LANES), 0)
    l_io = lax.broadcasted_iota(jnp.int32, (LANES, LANES), 1)
    lane = lax.broadcasted_iota(jnp.int32, (SUB, LANES), 1)
    innov = []
    for i in range(nb):
        first = a_ref[i, i, 0:SUB, :]
        pred = jnp.where(lane == 0, wide(first[1:2, LANES - 1:LANES]), wide(first[0:1, :]))
        innov.append(wide(values_ref[i:i + 1, :]) - pred)
        d = a_ref[i, i]
        below = jnp.where(r_io > l_io, d, 0.0)
        diag = jnp.where(r_io == l_io, d + variance_ref[i:i + 1, :], 0.0)
        a_ref[i, i] = below + below.T + diag
    for i in range(nb):
        for j in range(i + 1, nb):
            linv_ref[i * LANES:(i + 1) * LANES, j * LANES:(j + 1) * LANES] = jnp.zeros(
                (LANES, LANES), jnp.float32
            )
    for i in range(nb):
        x = jnp.concatenate(
            inverse_factor([a_ref[i, i, g * SUB:(g + 1) * SUB, :] for g in range(GROUPS)]), axis=0
        )
        at = slice(i * LANES, (i + 1) * LANES)
        for j in range(i + 1, nb):
            l_ref[j, i] = dot_dims(a_ref[j, i], x, 1, 1)
        for k in range(i + 1, nb):
            for j in range(k, nb):
                a_ref[j, k] = a_ref[j, k] - dot_dims(l_ref[j, i], l_ref[k, i], 1, 1)
        linv_ref[at, at] = x
        if i > 0:
            acc = dot(l_ref[i, 0], linv_ref[0:LANES, 0:i * LANES])
            for k in range(1, i):
                acc = acc + dot(l_ref[i, k], linv_ref[k * LANES:(k + 1) * LANES, 0:i * LANES])
            linv_ref[at, 0:i * LANES] = -dot(x, acc)
    white_ref[...] = dot_dims(jnp.concatenate(innov, axis=1), linv_ref[...], 1, 1)


def rows_kernel(got_ref, linv_ref, white_ref, mean_ref, gain_ref, after_ref, c_ref):
    plane = got_ref.shape[0]
    rows, m = gain_ref.shape
    own = rows // plane
    nb = m // LANES
    skip = got_ref.shape[1] - nb * own
    for i in range(plane):
        for j in range(nb):
            at = skip + j * own
            c_ref[i * own:(i + 1) * own, j * LANES:(j + 1) * LANES] = got_ref[i, at:at + own, :]
    gain = dot_dims(c_ref[...], linv_ref[...], 1, 1)
    gain_ref[...] = gain
    after_ref[...] = dot_dims(white_ref[...], gain, 1, 1) + mean_ref[...]


def update_kernel(at_ref, cov_ref, mine_ref, other_ref, linv_ref, gain_ref, out_ref, c_ref):
    n_z, halves, tall, _ = mine_ref.shape
    cols, m = c_ref.shape
    nb = m // LANES
    own = tall // nb
    core = at_ref[2]
    for ref, k in ((mine_ref, core), (other_ref, 1 - core)):
        start = pl.multiple_of(k * (n_z * own), n_z * own)
        for h in range(halves):
            for z in range(n_z):
                for j in range(nb):
                    at = h * (cols // halves) + z * own
                    c_ref[pl.ds(start + at, own), j * LANES:(j + 1) * LANES] = ref[
                        z, h, j * own:(j + 1) * own, :
                    ]
    gain_cols = dot_dims(c_ref[...], linv_ref[...], 1, 1)
    out_ref[...] = cov_ref[...] - dot_dims(gain_ref[...], gain_cols, 1, 1)


def on_device(covariance, state_mean, obs_values, obs_cells, obs_weights, obs_variance):
    rows, cols = covariance.shape
    n_row, n_col = lax.axis_size("row"), lax.axis_size("col")
    n_z = n_row // 2
    row, col = lax.axis_index("row"), lax.axis_index("col")
    core = lax.rem(row, 2)
    plane = 2 * n_col
    batches, _, obs = obs_cells.shape
    m = batches * obs
    nb = m // LANES
    own = rows // plane
    c_rows = own * nb
    s_rows = nb * (nb + 1) // 2 * LANES // plane
    chunk = s_rows + c_rows
    at = jnp.stack([row, col, core]).astype(jnp.int32)
    mean = state_mean.reshape(1, rows)

    plane_groups = [[z * plane + i for i in range(plane)] for z in range(n_z)]
    z_groups = [[2 * z + k for z in range(n_z)] for k in range(2)]
    pairs = []
    for idx in range(n_row * n_col):
        r, c = divmod(idx, n_col)
        z, k = divmod(r, 2)
        pairs.append((idx, (2 * c + k) * n_col + z))

    send = call(
        project_kernel,
        shape(plane, chunk, LANES),
        [SMEM, VMEM, VMEM, VMEM, VMEM],
        [pltpu.VMEM((rows, m), jnp.float32), pltpu.VMEM((m, m), jnp.float32)],
        flops=2 * rows * m * (cols + m),
        name="project",
    )(at, covariance, mean, obs_cells, obs_weights)
    got = lax.all_to_all(send, ("row", "col"), 0, 0, axis_index_groups=plane_groups)
    s_chunk = jnp.sum(got[:, :s_rows], axis=0)
    c_own = jnp.sum(got[:, s_rows:].reshape(2, n_col, c_rows, LANES), axis=1)

    s_send, c_own = lax.optimization_barrier(
        (jnp.broadcast_to(s_chunk[None], (n_z, s_rows, LANES)), c_own)
    )
    s_all = lax.all_to_all(s_send, "row", 0, 0, axis_index_groups=z_groups)
    s_all, c_own = lax.optimization_barrier((s_all, c_own))
    c_tr = lax.ppermute(c_own, ("row", "col"), pairs)
    s_full = jnp.sum(s_all, axis=0)
    send2 = jnp.concatenate(
        [
            jnp.broadcast_to(s_full[None], (plane, s_rows, LANES)),
            jnp.broadcast_to(c_own[:, None], (2, n_col, c_rows, LANES)).reshape(plane, c_rows, LANES),
        ],
        axis=1,
    )
    got2 = lax.all_to_all(send2, ("row", "col"), 0, 0, axis_index_groups=plane_groups)

    c_tr, got2 = lax.optimization_barrier((c_tr, got2))
    c_z = lax.all_to_all(
        jnp.broadcast_to(c_tr[None], (n_z,) + c_tr.shape), "row", 0, 0, axis_index_groups=z_groups
    )
    linv, white = call(
        factor_kernel,
        (shape(m, m), shape(SUB, m)),
        [VMEM] * 3,
        [pltpu.VMEM((nb, nb, LANES, LANES), jnp.float32), pltpu.VMEM((nb, nb, LANES, LANES), jnp.float32)],
        flops=1 << 34,
        name="factor",
    )(got2, obs_values.reshape(nb, LANES), obs_variance.reshape(nb, LANES))
    c_z, linv = lax.optimization_barrier((c_z, linv))
    c_other = lax.ppermute(c_z, "row", [(i, i ^ 1) for i in range(n_row)])
    gain, after = call(
        rows_kernel,
        (shape(rows, m), shape(SUB, rows)),
        [VMEM] * 4,
        [pltpu.VMEM((rows, m), jnp.float32)],
        flops=1 << 31,
        name="rows",
    )(got2, linv, white, mean)
    updated = call(
        update_kernel,
        shape(rows, cols),
        [SMEM] + [VMEM] * 5,
        [pltpu.VMEM((cols, m), jnp.float32)],
        flops=1 << 31,
        name="update",
    )(at, covariance, c_z, c_other, linv, gain)
    return (updated, after[0])


def solution(mesh):
    return jax.shard_map(
        on_device,
        mesh=mesh,
        in_specs=(P("row", "col"), P("row"), P(), P(), P(), P()),
        out_specs=(P("row", "col"), P("row")),
        check_vma=False,
    )
```

```python
import jax
import jax.numpy as jnp
from jax import lax
from jax.experimental import pallas as pl
from jax.experimental.pallas import tpu as pltpu
from jax.sharding import PartitionSpec as P

SUB = 8
LANES = 128
GROUPS = LANES // SUB
HI = lax.Precision.HIGHEST
HBM = pl.BlockSpec(memory_space=pltpu.HBM)
VMEM = pl.BlockSpec(memory_space=pltpu.VMEM)
SMEM = pl.BlockSpec(memory_space=pltpu.SMEM)
LIMIT = 48 * 1024 * 1024


def dot(a, b):
    return jnp.dot(a, b, precision=HI, preferred_element_type=jnp.float32)


def dot_dims(a, b, da, db):
    return lax.dot_general(
        a, b, (((da,), (db,)), ((), ())), precision=HI, preferred_element_type=jnp.float32
    )


def wide(x):
    return jnp.broadcast_to(x, (SUB, LANES))


def lower_blocks(n):
    return [(i, j) for i in range(n) for j in range(i + 1)]


def call(kernel, out_shape, specs, scratch=(), flops=0, name=None):
    return pl.pallas_call(
        kernel,
        out_shape=out_shape,
        in_specs=specs,
        out_specs=jax.tree.map(lambda _: VMEM, out_shape),
        scratch_shapes=list(scratch),
        compiler_params=pltpu.CompilerParams(vmem_limit_bytes=LIMIT),
        cost_estimate=pl.CostEstimate(flops=flops, bytes_accessed=1 << 20, transcendentals=0),
        name=name,
    )


def shape(*dims):
    return jax.ShapeDtypeStruct(dims, jnp.float32)


def operator(cells_ref, weights_ref, batch, start, count):
    foot, obs = cells_ref.shape[1], cells_ref.shape[2]
    positions = start + lax.broadcasted_iota(jnp.int32, (count, obs), 0)
    total = jnp.zeros((count, obs), jnp.float32)
    for f in range(foot):
        hit = cells_ref[batch, f:f + 1, :] == positions
        total = total + jnp.where(hit, weights_ref[batch, f:f + 1, :], 0.0)
    return total


def project_kernel(
    at_ref, cov_in, mean_in, cells_in, weights_in, send_ref, c_ref, s_ref, cov_ref, mean_ref, cells_ref, weights_ref, sems
):
    moves = [
        pltpu.make_async_copy(src, dst, sems.at[n])
        for n, (src, dst) in enumerate(
            [(cells_in, cells_ref), (weights_in, weights_ref), (cov_in, cov_ref), (mean_in, mean_ref)]
        )
    ]
    for move in moves:
        move.start()
    for move in moves:
        move.wait()
    rows, cols = cov_ref.shape
    batches, _, obs = cells_ref.shape
    plane = send_ref.shape[0]
    nb = batches * obs // LANES
    per = obs // LANES
    row_ops = []
    cov = cov_ref[...]
    for b in range(batches):
        col_op = operator(cells_ref, weights_ref, b, at_ref[1] * cols, cols)
        row_ops.append(operator(cells_ref, weights_ref, b, at_ref[0] * rows, rows))
        c_ref[:, b * obs:(b + 1) * obs] = dot(cov, col_op)
    for i in range(batches):
        for j in range(i + 1):
            s_ref[i * obs:(i + 1) * obs, j * obs:(j + 1) * obs] = dot_dims(
                row_ops[i], c_ref[:, j * obs:(j + 1) * obs], 0, 0
            )
    low = lower_blocks(nb)
    tiles = len(low) * GROUPS // plane
    lane = lax.broadcasted_iota(jnp.int32, (SUB, LANES), 1)
    sub = lax.broadcasted_iota(jnp.int32, (SUB, LANES), 0)
    mean = jnp.broadcast_to(mean_ref[...], (SUB, rows))
    mean = jnp.where(at_ref[1] == 0, mean, 0.0)
    preds = [dot(mean, row_ops[b]) for b in range(batches)]
    for n, (i, j) in enumerate(low):
        for g in range(GROUPS):
            t = s_ref[i * LANES + g * SUB:i * LANES + (g + 1) * SUB, j * LANES:(j + 1) * LANES]
            if i == j and g == 0:
                p = preds[i // per][:, (i % per) * LANES:(i % per + 1) * LANES]
                t = jnp.where((sub == 0) & (lane > 0), p, t)
                t = jnp.where((sub == 1) & (lane == LANES - 1), wide(p[:, :1]), t)
            q = n * GROUPS + g
            send_ref[q // tiles, (q % tiles) * SUB:(q % tiles + 1) * SUB, :] = t
    own = rows // plane
    for i in range(plane):
        for j in range(nb):
            at = (tiles + j) * SUB
            send_ref[i, at:at + own, :] = c_ref[i * own:(i + 1) * own, j * LANES:(j + 1) * LANES]


def inverse_factor(v, jobs):
    v = list(v)
    lane = lax.broadcasted_iota(jnp.int32, (SUB, LANES), 1)
    sub = lax.broadcasted_iota(jnp.int32, (SUB, LANES), 0)
    out = []
    following = None
    for p in range(len(v)):
        last = p + 1 == len(v)
        t = v[p]
        base = p * SUB
        inside = (lane >= base) & (lane < base + SUB)
        col = following or [wide(t[:, base + s:base + s + 1]) for s in range(SUB)]
        ahead, square = [], []
        if not last:
            nxt = base + SUB
            ahead = [wide(t[:, nxt + s:nxt + s + 1]) for s in range(SUB)]
            square = [wide(v[p + 1][:, nxt + s:nxt + s + 1]) for s in range(SUB)]
        t = jnp.where(inside, jnp.where(lane - base == sub, 1.0, 0.0), t)
        low = t
        piv = jnp.ones((SUB, LANES), jnp.float32)
        pairs = []
        for u in range(0, SUB, 2):
            a = wide(col[u][u:u + 1])
            b = wide(col[u + 1][u:u + 1])
            c = wide(col[u + 1][u + 1:u + 2])
            det = a * c - b * b
            rd = pltpu.reciprocal(det, approx=True)
            ra = pltpu.reciprocal(a, approx=True)
            here = (sub == u) | (sub == u + 1)
            c1 = jnp.where(here, 0.0, col[u])
            c2 = jnp.where(here, 0.0, col[u + 1])
            m1 = (c1 * c - c2 * b) * rd
            m2 = (c2 * a - c1 * b) * rd

            def clear(z):
                return z - (m1 * wide(z[u:u + 1]) + m2 * wide(z[u + 1:u + 2]))

            for w in range(u + 2, SUB):
                col[w] = clear(col[w])
            ahead = [clear(z) for z in ahead]
            t = clear(t)
            low = jnp.where(
                sub > u + 1, clear(low), jnp.where(sub == u + 1, low - (b * ra) * wide(low[u:u + 1]), low)
            )
            piv = jnp.where(sub == u, a, jnp.where(sub == u + 1, det * ra, piv))
            pairs.append((a * rd, b * rd, c * rd))
        out.append(jnp.where(lane <= sub + base, low * lax.rsqrt(piv), 0.0))

        def solved(z):
            q = []
            for u in range(0, SUB, 2):
                ar, br, cr = pairs[u // 2]
                z0, z1 = wide(z[u:u + 1]), wide(z[u + 1:u + 2])
                q.extend((z0 * cr - z1 * br, z1 * ar - z0 * br))
            return q

        def less(w, c, q):
            g = [c[s] * q[s] for s in range(SUB)]
            return w - (((g[0] + g[1]) + (g[2] + g[3])) + ((g[4] + g[5]) + (g[6] + g[7])))

        if not last:
            q = solved(t)
            following = None
            for j in range(p + 1, len(v)):
                c = [wide(v[j][:, base + s:base + s + 1]) for s in range(SUB)]
                v[j] = less(jnp.where(inside, 0.0, v[j]), c, q)
                if following is None:
                    following = [less(square[s], c, solved(ahead[s])) for s in range(SUB)]
        if jobs:
            jobs.pop(0)()
    while jobs:
        jobs.pop(0)()
    return jnp.concatenate(out, axis=0)


def factor_kernel(
    got_ref, values_ref, variance_ref, mean_ref, linv_ref, gain_ref, after_ref, a_ref, l_ref, e_ref, y_ref
):
    nb = values_ref.shape[0]
    rows = gain_ref.shape[0]
    low = lower_blocks(nb)
    plane = got_ref.shape[0]
    tiles = len(low) * GROUPS // plane
    own = rows // plane
    for n, (i, j) in enumerate(low):
        for g in range(GROUPS):
            q = n * GROUPS + g
            a_ref[i, j, g * SUB:(g + 1) * SUB, :] = got_ref[
                q // tiles, (q % tiles) * SUB:(q % tiles + 1) * SUB, :
            ]
    for i in range(plane):
        for j in range(nb):
            at = tiles * SUB + j * own
            e_ref[j, i * own:(i + 1) * own, :] = got_ref[i, at:at + own, :]
    r_io = lax.broadcasted_iota(jnp.int32, (LANES, LANES), 0)
    l_io = lax.broadcasted_iota(jnp.int32, (LANES, LANES), 1)
    lane = lax.broadcasted_iota(jnp.int32, (SUB, LANES), 1)
    for i in range(nb):
        first = a_ref[i, i, 0:SUB, :]
        pred = jnp.where(lane == 0, wide(first[1:2, LANES - 1:LANES]), wide(first[0:1, :]))
        e_ref[i, rows:rows + SUB, :] = wide(values_ref[i:i + 1, :]) - pred
        d = a_ref[i, i]
        below = jnp.where(r_io > l_io, d, 0.0)
        diag = jnp.where(r_io == l_io, d + variance_ref[i:i + 1, :], 0.0)
        a_ref[i, i] = below + below.T + diag
    for i in range(nb):
        for j in range(i + 1, nb):
            linv_ref[i * LANES:(i + 1) * LANES, j * LANES:(j + 1) * LANES] = jnp.zeros(
                (LANES, LANES), jnp.float32
            )

    def span(i):
        return slice(i * LANES, (i + 1) * LANES)

    def scale(j, i, x):
        l_ref[j, i] = dot_dims(a_ref[j, i], x, 1, 1)

    def reduce(j, k, i):
        a_ref[j, k] = a_ref[j, k] - dot_dims(l_ref[j, i], l_ref[k, i], 1, 1)

    def scale_rows(i, x):
        e_ref[i] = dot_dims(e_ref[i], x, 1, 1)

    def reduce_rows(k, i):
        e_ref[k] = e_ref[k] - dot_dims(e_ref[i], l_ref[k, i], 1, 1)

    def gather(i):
        acc = dot(l_ref[i, 0], linv_ref[0:LANES, 0:i * LANES])
        for k in range(1, i):
            acc = acc + dot(l_ref[i, k], linv_ref[span(k), 0:i * LANES])
        y_ref[:, 0:i * LANES] = acc

    def finish(i):
        linv_ref[span(i), 0:i * LANES] = -dot(linv_ref[span(i), span(i)], y_ref[:, 0:i * LANES])

    def work(f, *args):
        return lambda: f(*args)

    jobs = []
    for i in range(nb):
        x = inverse_factor([a_ref[i, i, g * SUB:(g + 1) * SUB, :] for g in range(GROUPS)], jobs)
        linv_ref[span(i), span(i)] = x
        if i + 1 < nb:
            scale(i + 1, i, x)
            reduce(i + 1, i + 1, i)
            for j in range(i + 2, nb):
                jobs.append(work(scale, j, i, x))
            for k in range(i + 1, nb):
                for j in range(max(k, i + 2), nb):
                    jobs.append(work(reduce, j, k, i))
            jobs.append(work(scale_rows, i, x))
            for k in range(i + 1, nb):
                jobs.append(work(reduce_rows, k, i))
            if i > 0:
                jobs.append(work(finish, i))
            jobs.append(work(gather, i + 1))
        else:
            scale_rows(i, x)
            finish(i)
    for i in range(nb):
        gain_ref[:, span(i)] = e_ref[i, 0:rows, :]
    after = mean_ref[...]
    for i in range(nb):
        after = after + dot_dims(e_ref[i, rows:rows + SUB, :], e_ref[i, 0:rows, :], 1, 1)
    after_ref[...] = after


def update_kernel(cov_ref, pieces_ref, linv_ref, gain_ref, out_ref, c_ref):
    n_row, halves, tall, _ = pieces_ref.shape
    cols, m = c_ref.shape
    nb = m // LANES
    own = tall // nb
    for h in range(halves):
        for r in range(n_row):
            z, k = divmod(r, 2)
            at = h * (cols // halves) + (k * (n_row // 2) + z) * own
            for j in range(nb):
                c_ref[at:at + own, j * LANES:(j + 1) * LANES] = pieces_ref[r, h, j * own:(j + 1) * own, :]
    gain_cols = dot_dims(c_ref[...], linv_ref[...], 1, 1)
    out_ref[...] = cov_ref[...] - dot_dims(gain_ref[...], gain_cols, 1, 1)


def on_device(covariance, state_mean, obs_values, obs_cells, obs_weights, obs_variance):
    rows, cols = covariance.shape
    n_row, n_col = lax.axis_size("row"), lax.axis_size("col")
    n_z = n_row // 2
    row, col = lax.axis_index("row"), lax.axis_index("col")
    plane = 2 * n_col
    batches, _, obs = obs_cells.shape
    m = batches * obs
    nb = m // LANES
    own = rows // plane
    c_rows = own * nb
    s_rows = nb * (nb + 1) // 2 * LANES // plane
    chunk = s_rows + c_rows
    at = jnp.stack([row, col]).astype(jnp.int32)
    mean = state_mean.reshape(1, rows)

    plane_groups = [[z * plane + i for i in range(plane)] for z in range(n_z)]
    z_groups = [[2 * z + k for z in range(n_z)] for k in range(2)]
    pairs = []
    for idx in range(n_row * n_col):
        r, c = divmod(idx, n_col)
        z, k = divmod(r, 2)
        pairs.append((idx, (2 * c + k) * n_col + z))

    send = call(
        project_kernel,
        shape(plane, chunk, LANES),
        [SMEM] + [HBM] * 4,
        [
            pltpu.VMEM((rows, m), jnp.float32),
            pltpu.VMEM((m, m), jnp.float32),
            pltpu.VMEM((rows, cols), jnp.float32),
            pltpu.VMEM((1, rows), jnp.float32),
            pltpu.VMEM(obs_cells.shape, jnp.int32),
            pltpu.VMEM(obs_weights.shape, jnp.float32),
            pltpu.SemaphoreType.DMA((4,)),
        ],
        flops=2 * rows * m * (cols + m),
        name="project",
    )(at, covariance, mean, obs_cells, obs_weights)
    got = lax.all_to_all(send, ("row", "col"), 0, 0, axis_index_groups=plane_groups)
    s_chunk = jnp.sum(got[:, :s_rows], axis=0)
    c_own = jnp.sum(got[:, s_rows:].reshape(2, n_col, c_rows, LANES), axis=1)

    s_send = jnp.broadcast_to(s_chunk[None], (n_z, s_rows, LANES))
    c_tr = lax.ppermute(c_own, ("row", "col"), pairs)
    s_all = lax.all_to_all(s_send, "row", 0, 0, axis_index_groups=z_groups)
    c_cols = lax.all_gather(c_tr, "row")
    s_full = jnp.sum(s_all, axis=0)
    send2 = jnp.concatenate(
        [
            jnp.broadcast_to(s_full[None], (plane, s_rows, LANES)),
            jnp.broadcast_to(c_own[:, None], (2, n_col, c_rows, LANES)).reshape(plane, c_rows, LANES),
        ],
        axis=1,
    )
    got2 = lax.all_to_all(send2, ("row", "col"), 0, 0, axis_index_groups=plane_groups)
    linv, gain, after = call(
        factor_kernel,
        (shape(m, m), shape(rows, m), shape(SUB, rows)),
        [VMEM] * 4,
        [
            pltpu.VMEM((nb, nb, LANES, LANES), jnp.float32),
            pltpu.VMEM((nb, nb, LANES, LANES), jnp.float32),
            pltpu.VMEM((nb, rows + SUB, LANES), jnp.float32),
            pltpu.VMEM((LANES, m), jnp.float32),
        ],
        flops=1 << 20,
        name="factor",
    )(got2, obs_values.reshape(nb, LANES), obs_variance.reshape(nb, LANES), mean)
    updated = call(
        update_kernel,
        shape(rows, cols),
        [VMEM] * 4,
        [pltpu.VMEM((cols, m), jnp.float32)],
        flops=1 << 31,
        name="update",
    )(covariance, c_cols, linv, gain)
    return (updated, after[0])


def solution(mesh):
    return jax.shard_map(
        on_device,
        mesh=mesh,
        in_specs=(P("row", "col"), P("row"), P(), P(), P(), P()),
        out_specs=(P("row", "col"), P("row")),
        check_vma=False,
    )
```

```python
import jax
import jax.numpy as jnp
from jax import lax
from jax.experimental import pallas as pl
from jax.experimental.pallas import tpu as pltpu
from jax.sharding import PartitionSpec as P

SUB = 8
LANES = 128
GROUPS = LANES // SUB
HI = lax.Precision.HIGHEST
HBM = pl.BlockSpec(memory_space=pltpu.HBM)
VMEM = pl.BlockSpec(memory_space=pltpu.VMEM)
SMEM = pl.BlockSpec(memory_space=pltpu.SMEM)
LIMIT = 48 * 1024 * 1024


def dot(a, b):
    return jnp.dot(a, b, precision=HI, preferred_element_type=jnp.float32)


def dot_dims(a, b, da, db):
    return lax.dot_general(
        a, b, (((da,), (db,)), ((), ())), precision=HI, preferred_element_type=jnp.float32
    )


def wide(x):
    return jnp.broadcast_to(x, (SUB, LANES))


def lower_blocks(n):
    return [(i, j) for i in range(n) for j in range(i + 1)]


def call(kernel, out_shape, specs, scratch=(), flops=0, name=None, aliases=None, limit=LIMIT):
    return pl.pallas_call(
        kernel,
        out_shape=out_shape,
        in_specs=specs,
        out_specs=jax.tree.map(lambda _: VMEM, out_shape),
        scratch_shapes=list(scratch),
        input_output_aliases=aliases or {},
        compiler_params=pltpu.CompilerParams(vmem_limit_bytes=limit),
        cost_estimate=pl.CostEstimate(flops=flops, bytes_accessed=1 << 20, transcendentals=0),
        name=name,
    )


def shape(*dims):
    return jax.ShapeDtypeStruct(dims, jnp.float32)


def operator(cells_ref, weights_ref, batch, start, count):
    foot, obs = cells_ref.shape[1], cells_ref.shape[2]
    positions = start + lax.broadcasted_iota(jnp.int32, (count, obs), 0)
    total = jnp.zeros((count, obs), jnp.float32)
    for f in range(foot):
        hit = cells_ref[batch, f:f + 1, :] == positions
        total = total + jnp.where(hit, weights_ref[batch, f:f + 1, :], 0.0)
    return total


def project_kernel(
    at_ref, cov_in, mean_in, cells_in, weights_in, send_ref, c_ref, s_ref, cov_ref, mean_ref, cells_ref, weights_ref, sems
):
    moves = [
        pltpu.make_async_copy(src, dst, sems.at[n])
        for n, (src, dst) in enumerate(
            [(cells_in, cells_ref), (weights_in, weights_ref), (cov_in, cov_ref), (mean_in, mean_ref)]
        )
    ]
    for move in moves:
        move.start()
    for move in moves:
        move.wait()
    rows, cols = cov_ref.shape
    batches, _, obs = cells_ref.shape
    plane = send_ref.shape[0]
    nb = batches * obs // LANES
    per = obs // LANES
    row_ops = []
    cov = cov_ref[...]
    for b in range(batches):
        col_op = operator(cells_ref, weights_ref, b, at_ref[1] * cols, cols)
        row_ops.append(operator(cells_ref, weights_ref, b, at_ref[0] * rows, rows))
        c_ref[:, b * obs:(b + 1) * obs] = dot(cov, col_op)
    for i in range(batches):
        for j in range(i + 1):
            s_ref[i * obs:(i + 1) * obs, j * obs:(j + 1) * obs] = dot_dims(
                row_ops[i], c_ref[:, j * obs:(j + 1) * obs], 0, 0
            )
    low = lower_blocks(nb)
    tiles = len(low) * GROUPS // plane
    lane = lax.broadcasted_iota(jnp.int32, (SUB, LANES), 1)
    sub = lax.broadcasted_iota(jnp.int32, (SUB, LANES), 0)
    mean = jnp.broadcast_to(mean_ref[...], (SUB, rows))
    mean = jnp.where(at_ref[1] == 0, mean, 0.0)
    preds = [dot(mean, row_ops[b]) for b in range(batches)]
    for n, (i, j) in enumerate(low):
        for g in range(GROUPS):
            t = s_ref[i * LANES + g * SUB:i * LANES + (g + 1) * SUB, j * LANES:(j + 1) * LANES]
            if i == j and g == 0:
                p = preds[i // per][:, (i % per) * LANES:(i % per + 1) * LANES]
                t = jnp.where((sub == 0) & (lane > 0), p, t)
                t = jnp.where((sub == 1) & (lane == LANES - 1), wide(p[:, :1]), t)
            q = n * GROUPS + g
            send_ref[q // tiles, (q % tiles) * SUB:(q % tiles + 1) * SUB, :] = t
    own = rows // plane
    for i in range(plane):
        for j in range(nb):
            at = (tiles + j) * SUB
            send_ref[i, at:at + own, :] = c_ref[i * own:(i + 1) * own, j * LANES:(j + 1) * LANES]


def inverse_factor(v, jobs):
    v = list(v)
    lane = lax.broadcasted_iota(jnp.int32, (SUB, LANES), 1)
    sub = lax.broadcasted_iota(jnp.int32, (SUB, LANES), 0)
    out = []
    following = None
    for p in range(len(v)):
        last = p + 1 == len(v)
        t = v[p]
        base = p * SUB
        inside = (lane >= base) & (lane < base + SUB)
        col = following or [wide(t[:, base + s:base + s + 1]) for s in range(SUB)]
        ahead, square = [], []
        if not last:
            nxt = base + SUB
            ahead = [wide(t[:, nxt + s:nxt + s + 1]) for s in range(SUB)]
            square = [wide(v[p + 1][:, nxt + s:nxt + s + 1]) for s in range(SUB)]
        t = jnp.where(inside, jnp.where(lane - base == sub, 1.0, 0.0), t)
        low = t
        piv = jnp.ones((SUB, LANES), jnp.float32)
        pairs = []
        for u in range(0, SUB, 2):
            a = wide(col[u][u:u + 1])
            b = wide(col[u + 1][u:u + 1])
            c = wide(col[u + 1][u + 1:u + 2])
            det = a * c - b * b
            rd = pltpu.reciprocal(det, approx=True)
            ra = pltpu.reciprocal(a, approx=True)
            here = (sub == u) | (sub == u + 1)
            c1 = jnp.where(here, 0.0, col[u])
            c2 = jnp.where(here, 0.0, col[u + 1])
            m1 = (c1 * c - c2 * b) * rd
            m2 = (c2 * a - c1 * b) * rd

            def clear(z):
                return z - (m1 * wide(z[u:u + 1]) + m2 * wide(z[u + 1:u + 2]))

            for w in range(u + 2, SUB):
                col[w] = clear(col[w])
            ahead = [clear(z) for z in ahead]
            t = clear(t)
            low = jnp.where(
                sub > u + 1, clear(low), jnp.where(sub == u + 1, low - (b * ra) * wide(low[u:u + 1]), low)
            )
            piv = jnp.where(sub == u, a, jnp.where(sub == u + 1, det * ra, piv))
            pairs.append((a * rd, b * rd, c * rd))
        out.append(jnp.where(lane <= sub + base, low * lax.rsqrt(piv), 0.0))

        def solved(z):
            q = []
            for u in range(0, SUB, 2):
                ar, br, cr = pairs[u // 2]
                z0, z1 = wide(z[u:u + 1]), wide(z[u + 1:u + 2])
                q.extend((z0 * cr - z1 * br, z1 * ar - z0 * br))
            return q

        def less(w, c, q):
            g = [c[s] * q[s] for s in range(SUB)]
            return w - (((g[0] + g[1]) + (g[2] + g[3])) + ((g[4] + g[5]) + (g[6] + g[7])))

        if not last:
            q = solved(t)
            following = None
            for j in range(p + 1, len(v)):
                c = [wide(v[j][:, base + s:base + s + 1]) for s in range(SUB)]
                v[j] = less(jnp.where(inside, 0.0, v[j]), c, q)
                if following is None:
                    following = [less(square[s], c, solved(ahead[s])) for s in range(SUB)]
        if jobs:
            jobs.pop(0)()
    while jobs:
        jobs.pop(0)()
    return jnp.concatenate(out, axis=0)


def prepare(got_ref, values_ref, variance_ref, linv_ref, a_ref, e_ref):
    nb = values_ref.shape[0]
    rows = e_ref.shape[1] - SUB
    low = lower_blocks(nb)
    plane = got_ref.shape[0]
    tiles = len(low) * GROUPS // plane
    own = rows // plane
    for n, (i, j) in enumerate(low):
        for g in range(GROUPS):
            q = n * GROUPS + g
            a_ref[i, j, g * SUB:(g + 1) * SUB, :] = got_ref[
                q // tiles, (q % tiles) * SUB:(q % tiles + 1) * SUB, :
            ]
    for i in range(plane):
        for j in range(nb):
            at = tiles * SUB + j * own
            e_ref[j, i * own:(i + 1) * own, :] = got_ref[i, at:at + own, :]
    r_io = lax.broadcasted_iota(jnp.int32, (LANES, LANES), 0)
    l_io = lax.broadcasted_iota(jnp.int32, (LANES, LANES), 1)
    lane = lax.broadcasted_iota(jnp.int32, (SUB, LANES), 1)
    for i in range(nb):
        first = a_ref[i, i, 0:SUB, :]
        pred = jnp.where(lane == 0, wide(first[1:2, LANES - 1:LANES]), wide(first[0:1, :]))
        e_ref[i, rows:rows + SUB, :] = wide(values_ref[i:i + 1, :]) - pred
        d = a_ref[i, i]
        below = jnp.where(r_io > l_io, d, 0.0)
        diag = jnp.where(r_io == l_io, d + variance_ref[i:i + 1, :], 0.0)
        a_ref[i, i] = below + below.T + diag
    for i in range(nb):
        for j in range(i + 1, nb):
            linv_ref[i * LANES:(i + 1) * LANES, j * LANES:(j + 1) * LANES] = jnp.zeros(
                (LANES, LANES), jnp.float32
            )


def factor_steps(begin, end, linv_ref, a_ref, l_ref, e_ref, y_ref):
    nb = a_ref.shape[0]

    def span(i):
        return slice(i * LANES, (i + 1) * LANES)

    def scale(j, i):
        l_ref[j, i] = dot_dims(a_ref[j, i], linv_ref[span(i), span(i)], 1, 1)

    def reduce(j, k, i):
        a_ref[j, k] = a_ref[j, k] - dot_dims(l_ref[j, i], l_ref[k, i], 1, 1)

    def scale_rows(i):
        e_ref[i] = dot_dims(e_ref[i], linv_ref[span(i), span(i)], 1, 1)

    def reduce_rows(k, i):
        e_ref[k] = e_ref[k] - dot_dims(e_ref[i], l_ref[k, i], 1, 1)

    def gather(i):
        acc = dot(l_ref[i, 0], linv_ref[0:LANES, 0:i * LANES])
        for k in range(1, i):
            acc = acc + dot(l_ref[i, k], linv_ref[span(k), 0:i * LANES])
        y_ref[:, 0:i * LANES] = acc

    def finish(i):
        linv_ref[span(i), 0:i * LANES] = -dot(linv_ref[span(i), span(i)], y_ref[:, 0:i * LANES])

    def work(f, *args):
        return lambda: f(*args)

    def rest(i):
        todo = [work(scale, j, i) for j in range(i + 2, nb)]
        todo += [work(reduce, j, k, i) for k in range(i + 1, nb) for j in range(max(k, i + 2), nb)]
        todo.append(work(scale_rows, i))
        todo += [work(reduce_rows, k, i) for k in range(i + 1, nb)]
        if i > 0:
            todo.append(work(finish, i))
        todo.append(work(gather, i + 1))
        return todo

    for i in range(begin, end):
        jobs = rest(i - 1) if i > 0 else []
        linv_ref[span(i), span(i)] = inverse_factor(
            [a_ref[i, i, g * SUB:(g + 1) * SUB, :] for g in range(GROUPS)], jobs
        )
        if i + 1 < nb:
            scale(i + 1, i)
            reduce(i + 1, i + 1, i)
        else:
            scale_rows(i)
            finish(i)


def early_kernel(got_ref, values_ref, variance_ref, linv_ref, a_ref, l_ref, e_ref, y_ref):
    prepare(got_ref, values_ref, variance_ref, linv_ref, a_ref, e_ref)
    factor_steps(0, a_ref.shape[0] - 1, linv_ref, a_ref, l_ref, e_ref, y_ref)


def late_kernel(
    mean_ref, linv_in, a_in, l_in, e_in, y_in, linv_ref, a_ref, l_ref, e_ref, y_ref, after_ref
):
    nb = a_ref.shape[0]
    rows = e_ref.shape[1] - SUB
    factor_steps(nb - 1, nb, linv_ref, a_ref, l_ref, e_ref, y_ref)
    after = mean_ref[...]
    for i in range(nb):
        after = after + dot_dims(e_ref[i, rows:rows + SUB, :], e_ref[i, 0:rows, :], 1, 1)
    after_ref[...] = after


def update_kernel(at_ref, cov_ref, mine_ref, other_ref, linv_ref, e_ref, out_ref, c_ref):
    n_z, halves, tall, _ = mine_ref.shape
    rows, cols = cov_ref.shape
    m = c_ref.shape[1]
    nb = m // LANES
    own = tall // nb
    core = lax.rem(at_ref[0], 2)
    z_here = lax.div(at_ref[0], 2)
    for ref, k in ((mine_ref, core), (other_ref, 1 - core)):
        for d in range(n_z):
            start = pl.multiple_of((k * n_z + lax.bitwise_xor(z_here, d)) * own, own)
            for h in range(halves):
                for j in range(nb):
                    c_ref[pl.ds(start + h * (cols // halves), own), j * LANES:(j + 1) * LANES] = ref[
                        d, h, j * own:(j + 1) * own, :
                    ]
    gain_cols = dot_dims(c_ref[...], linv_ref[...], 1, 1)
    gain = jnp.concatenate([e_ref[j, 0:rows, :] for j in range(nb)], axis=1)
    out_ref[...] = cov_ref[...] - dot_dims(gain, gain_cols, 1, 1)


def on_device(covariance, state_mean, obs_values, obs_cells, obs_weights, obs_variance):
    rows, cols = covariance.shape
    n_row, n_col = lax.axis_size("row"), lax.axis_size("col")
    n_z = n_row // 2
    row, col = lax.axis_index("row"), lax.axis_index("col")
    plane = 2 * n_col
    batches, _, obs = obs_cells.shape
    m = batches * obs
    nb = m // LANES
    own = rows // plane
    c_rows = own * nb
    s_rows = nb * (nb + 1) // 2 * LANES // plane
    chunk = s_rows + c_rows
    at = jnp.stack([row, col]).astype(jnp.int32)
    mean = state_mean.reshape(1, rows)

    plane_groups = [[z * plane + i for i in range(plane)] for z in range(n_z)]
    z_groups = [[2 * z + k for z in range(n_z)] for k in range(2)]
    pairs = []
    for idx in range(n_row * n_col):
        r, c = divmod(idx, n_col)
        z, k = divmod(r, 2)
        pairs.append((idx, (2 * c + k) * n_col + z))

    send = call(
        project_kernel,
        shape(plane, chunk, LANES),
        [SMEM] + [HBM] * 4,
        [
            pltpu.VMEM((rows, m), jnp.float32),
            pltpu.VMEM((m, m), jnp.float32),
            pltpu.VMEM((rows, cols), jnp.float32),
            pltpu.VMEM((1, rows), jnp.float32),
            pltpu.VMEM(obs_cells.shape, jnp.int32),
            pltpu.VMEM(obs_weights.shape, jnp.float32),
            pltpu.SemaphoreType.DMA((4,)),
        ],
        flops=2 * rows * m * (cols + m),
        name="project",
        limit=60 * 1024 * 1024,
    )(at, covariance, mean, obs_cells, obs_weights)
    got = lax.all_to_all(send, ("row", "col"), 0, 0, axis_index_groups=plane_groups)
    s_chunk = jnp.sum(got[:, :s_rows], axis=0)
    c_own = jnp.sum(got[:, s_rows:].reshape(2, n_col, c_rows, LANES), axis=1)

    s_send = jnp.broadcast_to(s_chunk[None], (n_z, s_rows, LANES))
    c_tr = lax.ppermute(c_own, ("row", "col"), pairs)
    s_all = lax.all_to_all(s_send, "row", 0, 0, axis_index_groups=z_groups)
    s_full = jnp.sum(s_all, axis=0)
    send2 = jnp.concatenate(
        [
            jnp.broadcast_to(s_full[None], (plane, s_rows, LANES)),
            jnp.broadcast_to(c_own[:, None], (2, n_col, c_rows, LANES)).reshape(plane, c_rows, LANES),
        ],
        axis=1,
    )
    send2, c_tr = lax.optimization_barrier((send2, c_tr))
    got2 = lax.all_to_all(send2, ("row", "col"), 0, 0, axis_index_groups=plane_groups)

    def partner(x, bit):
        return lax.ppermute(x, "row", [(i, i ^ bit) for i in range(n_row)])

    pieces = c_tr[None]
    bits = []
    while 1 << len(bits) < n_z:
        bits.append(2 << len(bits))
    for bit in bits[:0:-1]:
        theirs = partner(pieces, bit)
        pieces = jnp.stack([pieces, theirs], axis=1).reshape((-1,) + c_tr.shape)
    got2, pieces = lax.optimization_barrier((got2, pieces))
    theirs = partner(pieces, bits[0])
    state = (
        shape(m, m),
        shape(nb, nb, LANES, LANES),
        shape(nb, nb, LANES, LANES),
        shape(nb, rows + SUB, LANES),
        shape(LANES, m),
    )
    held = call(early_kernel, state, [VMEM] * 3, flops=1 << 30, name="early")(
        got2, obs_values.reshape(nb, LANES), obs_variance.reshape(nb, LANES)
    )
    held, theirs = lax.optimization_barrier((held, theirs))
    pieces = jnp.stack([pieces, theirs], axis=1).reshape((-1,) + c_tr.shape)
    other = partner(pieces, 1)
    out = call(
        late_kernel,
        state + (shape(SUB, rows),),
        [VMEM] * 6,
        flops=1 << 30,
        name="late",
        aliases={n + 1: n for n in range(len(state))},
    )(mean, *held)
    linv, e, after = out[0], out[3], out[5]
    updated = call(
        update_kernel,
        shape(rows, cols),
        [SMEM] + [VMEM] * 5,
        [pltpu.VMEM((cols, m), jnp.float32)],
        flops=1 << 31,
        name="update",
    )(at, covariance, pieces, other, linv, e)
    return (updated, after[0])


def solution(mesh):
    return jax.shard_map(
        on_device,
        mesh=mesh,
        in_specs=(P("row", "col"), P("row"), P(), P(), P(), P()),
        out_specs=(P("row", "col"), P("row")),
        check_vma=False,
    )
```

```python
import jax
import jax.numpy as jnp
from jax import lax
from jax.experimental import pallas as pl
from jax.experimental.pallas import tpu as pltpu
from jax.sharding import PartitionSpec as P

SUB = 8
LANES = 128
GROUPS = LANES // SUB
HI = lax.Precision.HIGHEST
HBM = pl.BlockSpec(memory_space=pltpu.HBM)
VMEM = pl.BlockSpec(memory_space=pltpu.VMEM)
SMEM = pl.BlockSpec(memory_space=pltpu.SMEM)
LIMIT = 48 * 1024 * 1024


def dot(a, b):
    return jnp.dot(a, b, precision=HI, preferred_element_type=jnp.float32)


def dot_dims(a, b, da, db):
    return lax.dot_general(
        a, b, (((da,), (db,)), ((), ())), precision=HI, preferred_element_type=jnp.float32
    )


def wide(x):
    return jnp.broadcast_to(x, (SUB, LANES))


def lower_blocks(n):
    return [(i, j) for i in range(n) for j in range(i + 1)]


def call(kernel, out_shape, specs, scratch=(), flops=0, name=None, aliases=None, limit=LIMIT):
    return pl.pallas_call(
        kernel,
        out_shape=out_shape,
        in_specs=specs,
        out_specs=jax.tree.map(lambda _: VMEM, out_shape),
        scratch_shapes=list(scratch),
        input_output_aliases=aliases or {},
        compiler_params=pltpu.CompilerParams(vmem_limit_bytes=limit),
        cost_estimate=pl.CostEstimate(flops=flops, bytes_accessed=1 << 20, transcendentals=0),
        name=name,
    )


def shape(*dims):
    return jax.ShapeDtypeStruct(dims, jnp.float32)


def operator(cells_ref, weights_ref, batch, start, count):
    foot, obs = cells_ref.shape[1], cells_ref.shape[2]
    positions = start + lax.broadcasted_iota(jnp.int32, (count, obs), 0)
    total = jnp.zeros((count, obs), jnp.float32)
    for f in range(foot):
        hit = cells_ref[batch, f:f + 1, :] == positions
        total = total + jnp.where(hit, weights_ref[batch, f:f + 1, :], 0.0)
    return total


def project_kernel(
    at_ref, cov_in, mean_in, cells_in, weights_in, send_ref, c_ref, s_ref, cov_ref, mean_ref, cells_ref, weights_ref, sems
):
    moves = [
        pltpu.make_async_copy(src, dst, sems.at[n])
        for n, (src, dst) in enumerate(
            [(cells_in, cells_ref), (weights_in, weights_ref), (cov_in, cov_ref), (mean_in, mean_ref)]
        )
    ]
    for move in moves:
        move.start()
    for move in moves:
        move.wait()
    rows, cols = cov_ref.shape
    batches, _, obs = cells_ref.shape
    plane = send_ref.shape[0]
    nb = batches * obs // LANES
    per = obs // LANES
    row_ops = []
    cov = cov_ref[...]
    for b in range(batches):
        col_op = operator(cells_ref, weights_ref, b, at_ref[1] * cols, cols)
        row_ops.append(operator(cells_ref, weights_ref, b, at_ref[0] * rows, rows))
        c_ref[:, b * obs:(b + 1) * obs] = dot(cov, col_op)
    for i in range(batches):
        for j in range(i + 1):
            s_ref[i * obs:(i + 1) * obs, j * obs:(j + 1) * obs] = dot_dims(
                row_ops[i], c_ref[:, j * obs:(j + 1) * obs], 0, 0
            )
    low = lower_blocks(nb)
    tiles = len(low) * GROUPS // plane
    lane = lax.broadcasted_iota(jnp.int32, (SUB, LANES), 1)
    sub = lax.broadcasted_iota(jnp.int32, (SUB, LANES), 0)
    mean = jnp.broadcast_to(mean_ref[...], (SUB, rows))
    mean = jnp.where(at_ref[1] == 0, mean, 0.0)
    preds = [dot(mean, row_ops[b]) for b in range(batches)]
    for n, (i, j) in enumerate(low):
        for g in range(GROUPS):
            t = s_ref[i * LANES + g * SUB:i * LANES + (g + 1) * SUB, j * LANES:(j + 1) * LANES]
            if i == j and g == 0:
                p = preds[i // per][:, (i % per) * LANES:(i % per + 1) * LANES]
                t = jnp.where((sub == 0) & (lane > 0), p, t)
                t = jnp.where((sub == 1) & (lane == LANES - 1), wide(p[:, :1]), t)
            q = n * GROUPS + g
            send_ref[q // tiles, (q % tiles) * SUB:(q % tiles + 1) * SUB, :] = t
    own = rows // plane
    for i in range(plane):
        for j in range(nb):
            at = (tiles + j) * SUB
            send_ref[i, at:at + own, :] = c_ref[i * own:(i + 1) * own, j * LANES:(j + 1) * LANES]


def inverse_factor(v, jobs):
    v = list(v)
    lane = lax.broadcasted_iota(jnp.int32, (SUB, LANES), 1)
    sub = lax.broadcasted_iota(jnp.int32, (SUB, LANES), 0)
    out = []
    following = None
    for p in range(len(v)):
        last = p + 1 == len(v)
        t = v[p]
        base = p * SUB
        inside = (lane >= base) & (lane < base + SUB)
        col = following or [wide(t[:, base + s:base + s + 1]) for s in range(SUB)]
        ahead, square = [], []
        if not last:
            nxt = base + SUB
            ahead = [wide(t[:, nxt + s:nxt + s + 1]) for s in range(SUB)]
            square = [wide(v[p + 1][:, nxt + s:nxt + s + 1]) for s in range(SUB)]
        t = jnp.where(inside, jnp.where(lane - base == sub, 1.0, 0.0), t)
        low = t
        piv = jnp.ones((SUB, LANES), jnp.float32)
        pairs = []
        for u in range(0, SUB, 2):
            a = wide(col[u][u:u + 1])
            b = wide(col[u + 1][u:u + 1])
            c = wide(col[u + 1][u + 1:u + 2])
            det = a * c - b * b
            rd = pltpu.reciprocal(det, approx=True)
            ra = pltpu.reciprocal(a, approx=True)
            here = (sub == u) | (sub == u + 1)
            c1 = jnp.where(here, 0.0, col[u])
            c2 = jnp.where(here, 0.0, col[u + 1])
            m1 = (c1 * c - c2 * b) * rd
            m2 = (c2 * a - c1 * b) * rd

            def clear(z):
                return z - (m1 * wide(z[u:u + 1]) + m2 * wide(z[u + 1:u + 2]))

            for w in range(u + 2, SUB):
                col[w] = clear(col[w])
            ahead = [clear(z) for z in ahead]
            t = clear(t)
            low = jnp.where(
                sub > u + 1, clear(low), jnp.where(sub == u + 1, low - (b * ra) * wide(low[u:u + 1]), low)
            )
            piv = jnp.where(sub == u, a, jnp.where(sub == u + 1, det * ra, piv))
            pairs.append((a * rd, b * rd, c * rd))
        out.append(jnp.where(lane <= sub + base, low * lax.rsqrt(piv), 0.0))

        def solved(z):
            q = []
            for u in range(0, SUB, 2):
                ar, br, cr = pairs[u // 2]
                z0, z1 = wide(z[u:u + 1]), wide(z[u + 1:u + 2])
                q.extend((z0 * cr - z1 * br, z1 * ar - z0 * br))
            return q

        def less(w, c, q):
            g = [c[s] * q[s] for s in range(SUB)]
            return w - (((g[0] + g[1]) + (g[2] + g[3])) + ((g[4] + g[5]) + (g[6] + g[7])))

        if not last:
            q = solved(t)
            following = None
            for j in range(p + 1, len(v)):
                c = [wide(v[j][:, base + s:base + s + 1]) for s in range(SUB)]
                v[j] = less(jnp.where(inside, 0.0, v[j]), c, q)
                if following is None:
                    following = [less(square[s], c, solved(ahead[s])) for s in range(SUB)]
        if jobs:
            jobs.pop(0)()
    while jobs:
        jobs.pop(0)()
    return jnp.concatenate(out, axis=0)


def prepare(got_ref, values_ref, variance_ref, linv_ref, a_ref, e_ref):
    nb = values_ref.shape[0]
    low = lower_blocks(nb)
    plane = got_ref.shape[0]
    tiles = len(low) * GROUPS // plane
    for n, (i, j) in enumerate(low):
        for g in range(GROUPS):
            q = n * GROUPS + g
            a_ref[i, j, g * SUB:(g + 1) * SUB, :] = got_ref[
                q // tiles, (q % tiles) * SUB:(q % tiles + 1) * SUB, :
            ]
    r_io = lax.broadcasted_iota(jnp.int32, (LANES, LANES), 0)
    l_io = lax.broadcasted_iota(jnp.int32, (LANES, LANES), 1)
    lane = lax.broadcasted_iota(jnp.int32, (SUB, LANES), 1)
    for i in range(nb):
        first = a_ref[i, i, 0:SUB, :]
        pred = jnp.where(lane == 0, wide(first[1:2, LANES - 1:LANES]), wide(first[0:1, :]))
        e_ref[i] = wide(values_ref[i:i + 1, :]) - pred
        d = a_ref[i, i]
        below = jnp.where(r_io > l_io, d, 0.0)
        diag = jnp.where(r_io == l_io, d + variance_ref[i:i + 1, :], 0.0)
        a_ref[i, i] = below + below.T + diag
    for i in range(nb):
        for j in range(i + 1, nb):
            linv_ref[i * LANES:(i + 1) * LANES, j * LANES:(j + 1) * LANES] = jnp.zeros(
                (LANES, LANES), jnp.float32
            )


def factor_steps(begin, end, linv_ref, a_ref, l_ref, e_ref, y_ref):
    nb = a_ref.shape[0]

    def span(i):
        return slice(i * LANES, (i + 1) * LANES)

    def scale(j, i):
        l_ref[j, i] = dot_dims(a_ref[j, i], linv_ref[span(i), span(i)], 1, 1)

    def reduce(j, k, i):
        a_ref[j, k] = a_ref[j, k] - dot_dims(l_ref[j, i], l_ref[k, i], 1, 1)

    def scale_rows(i):
        e_ref[i] = dot_dims(e_ref[i], linv_ref[span(i), span(i)], 1, 1)

    def reduce_rows(k, i):
        e_ref[k] = e_ref[k] - dot_dims(e_ref[i], l_ref[k, i], 1, 1)

    def gather(i):
        acc = dot(l_ref[i, 0], linv_ref[0:LANES, 0:i * LANES])
        for k in range(1, i):
            acc = acc + dot(l_ref[i, k], linv_ref[span(k), 0:i * LANES])
        y_ref[:, 0:i * LANES] = acc

    def finish(i):
        linv_ref[span(i), 0:i * LANES] = -dot(linv_ref[span(i), span(i)], y_ref[:, 0:i * LANES])

    def work(f, *args):
        return lambda: f(*args)

    def rest(i):
        todo = [work(scale, j, i) for j in range(i + 2, nb)]
        todo += [work(reduce, j, k, i) for k in range(i + 1, nb) for j in range(max(k, i + 2), nb)]
        todo.append(work(scale_rows, i))
        todo += [work(reduce_rows, k, i) for k in range(i + 1, nb)]
        if i > 0:
            todo.append(work(finish, i))
        todo.append(work(gather, i + 1))
        return todo

    for i in range(begin, end):
        jobs = rest(i - 1) if i > 0 else []
        linv_ref[span(i), span(i)] = inverse_factor(
            [a_ref[i, i, g * SUB:(g + 1) * SUB, :] for g in range(GROUPS)], jobs
        )
        if i + 1 < nb:
            scale(i + 1, i)
            reduce(i + 1, i + 1, i)
        else:
            scale_rows(i)
            finish(i)


def factor_kernel(got_ref, values_ref, variance_ref, linv_ref, e_ref, a_ref, l_ref, y_ref):
    prepare(got_ref, values_ref, variance_ref, linv_ref, a_ref, e_ref)
    factor_steps(0, a_ref.shape[0], linv_ref, a_ref, l_ref, e_ref, y_ref)


def gain_kernel(r_ref, mine_ref, linv_ref, e_ref, mean_ref, gain_ref, cols_ref, after_ref, c_ref):
    plane = r_ref.shape[0]
    rows, m = gain_ref.shape
    own = rows // plane
    nb = m // LANES
    skip = r_ref.shape[1] - nb * own
    arrange(mine_ref, c_ref)
    cols_ref[...] = dot_dims(c_ref[...], linv_ref[...], 1, 1)
    for i in range(plane):
        for j in range(nb):
            at = skip + j * own
            c_ref[i * own:(i + 1) * own, j * LANES:(j + 1) * LANES] = r_ref[i, at:at + own, :]
    gain = dot_dims(c_ref[...], linv_ref[...], 1, 1)
    gain_ref[...] = gain
    after = jnp.broadcast_to(mean_ref[...], (SUB, rows))
    for i in range(nb):
        after = after + dot_dims(e_ref[i], gain[:, i * LANES:(i + 1) * LANES], 1, 1)
    after_ref[...] = after[0:1]


def arrange(pieces_ref, c_ref):
    n_z, halves, tall, _ = pieces_ref.shape
    nb = c_ref.shape[1] // LANES
    own = tall // nb
    for h in range(halves):
        for z in range(n_z):
            at = (h * n_z + z) * own
            for j in range(nb):
                c_ref[at:at + own, j * LANES:(j + 1) * LANES] = pieces_ref[z, h, j * own:(j + 1) * own, :]


def update_kernel(at_ref, cov_ref, other_ref, mine_ref, linv_ref, gain_ref, out_ref, c_ref, g_ref):
    halves = other_ref.shape[1]
    part = c_ref.shape[0] // halves
    core = lax.rem(at_ref[0], 2)
    arrange(other_ref, c_ref)
    theirs = dot_dims(c_ref[...], linv_ref[...], 1, 1)
    for h in range(halves):
        for k, block in ((core, mine_ref[h * part:(h + 1) * part, :]), (1 - core, theirs[h * part:(h + 1) * part])):
            start = pl.multiple_of((2 * h + k) * part, part)
            g_ref[pl.ds(start, part), :] = block
    out_ref[...] = cov_ref[...] - dot_dims(gain_ref[...], g_ref[...], 1, 1)


def on_device(covariance, state_mean, obs_values, obs_cells, obs_weights, obs_variance):
    rows, cols = covariance.shape
    n_row, n_col = lax.axis_size("row"), lax.axis_size("col")
    n_z = n_row // 2
    row, col = lax.axis_index("row"), lax.axis_index("col")
    plane = 2 * n_col
    batches, _, obs = obs_cells.shape
    m = batches * obs
    nb = m // LANES
    own = rows // plane
    c_rows = own * nb
    s_rows = nb * (nb + 1) // 2 * LANES // plane
    chunk = s_rows + c_rows
    at = jnp.stack([row, col]).astype(jnp.int32)
    mean = state_mean.reshape(1, rows)

    plane_groups = [[z * plane + i for i in range(plane)] for z in range(n_z)]
    z_groups = [[2 * z + k for z in range(n_z)] for k in range(2)]
    pairs = []
    for idx in range(n_row * n_col):
        r, c = divmod(idx, n_col)
        z, k = divmod(r, 2)
        pairs.append((idx, (2 * c + k) * n_col + z))

    send = call(
        project_kernel,
        shape(plane, chunk, LANES),
        [SMEM] + [HBM] * 4,
        [
            pltpu.VMEM((rows, m), jnp.float32),
            pltpu.VMEM((m, m), jnp.float32),
            pltpu.VMEM((rows, cols), jnp.float32),
            pltpu.VMEM((1, rows), jnp.float32),
            pltpu.VMEM(obs_cells.shape, jnp.int32),
            pltpu.VMEM(obs_weights.shape, jnp.float32),
            pltpu.SemaphoreType.DMA((4,)),
        ],
        flops=2 * rows * m * (cols + m),
        name="project",
        limit=60 * 1024 * 1024,
    )(at, covariance, mean, obs_cells, obs_weights)
    got = lax.all_to_all(send, ("row", "col"), 0, 0, axis_index_groups=plane_groups)
    s_chunk = jnp.sum(got[:, :s_rows], axis=0)
    c_own = jnp.sum(got[:, s_rows:].reshape(2, n_col, c_rows, LANES), axis=1)

    s_send, c_own = lax.optimization_barrier(
        (jnp.broadcast_to(s_chunk[None], (n_z, s_rows, LANES)), c_own)
    )
    s_all = lax.all_to_all(s_send, "row", 0, 0, axis_index_groups=z_groups)
    s_all, c_own = lax.optimization_barrier((s_all, c_own))
    c_tr = lax.ppermute(c_own, ("row", "col"), pairs)
    send2 = jnp.concatenate(
        [
            jnp.broadcast_to(jnp.sum(s_all, axis=0)[None], (plane, s_rows, LANES)),
            jnp.broadcast_to(c_own[:, None], (2, n_col, c_rows, LANES)).reshape(plane, c_rows, LANES),
        ],
        axis=1,
    )
    got2 = lax.all_to_all(send2, ("row", "col"), 0, 0, axis_index_groups=plane_groups)
    got2, c_tr = lax.optimization_barrier((got2, c_tr))
    c_z = lax.all_to_all(
        jnp.broadcast_to(c_tr[None], (n_z,) + c_tr.shape), "row", 0, 0, axis_index_groups=z_groups
    )
    linv, white = call(
        factor_kernel,
        (shape(m, m), shape(nb, SUB, LANES)),
        [VMEM] * 3,
        [
            pltpu.VMEM((nb, nb, LANES, LANES), jnp.float32),
            pltpu.VMEM((nb, nb, LANES, LANES), jnp.float32),
            pltpu.VMEM((LANES, m), jnp.float32),
        ],
        flops=1 << 20,
        name="factor",
    )(got2, obs_values.reshape(nb, LANES), obs_variance.reshape(nb, LANES))
    c_z, linv = lax.optimization_barrier((c_z, linv))
    other = lax.ppermute(c_z, "row", [(i, i ^ 1) for i in range(n_row)])
    gain, gain_cols, after = call(
        gain_kernel,
        (shape(rows, m), shape(cols // 2, m), shape(1, rows)),
        [VMEM] * 5,
        [pltpu.VMEM((rows, m), jnp.float32)],
        flops=1 << 31,
        name="gain",
    )(got2, c_z, linv, white, mean)
    updated = call(
        update_kernel,
        shape(rows, cols),
        [SMEM] + [VMEM] * 5,
        [pltpu.VMEM((cols // 2, m), jnp.float32), pltpu.VMEM((cols, m), jnp.float32)],
        flops=1 << 31,
        name="update",
    )(at, covariance, other, gain_cols, linv, gain)
    return (updated, after.reshape(rows))


def solution(mesh):
    return jax.shard_map(
        on_device,
        mesh=mesh,
        in_specs=(P("row", "col"), P("row"), P(), P(), P(), P()),
        out_specs=(P("row", "col"), P("row")),
        check_vma=False,
    )
```

```python
import jax
import jax.numpy as jnp
from jax import lax
from jax.experimental import pallas as pl
from jax.experimental.pallas import tpu as pltpu
from jax.sharding import PartitionSpec as P

SUB = 8
LANES = 128
GROUPS = LANES // SUB
HI = lax.Precision.HIGHEST
HBM = pl.BlockSpec(memory_space=pltpu.HBM)
VMEM = pl.BlockSpec(memory_space=pltpu.VMEM)
SMEM = pl.BlockSpec(memory_space=pltpu.SMEM)
LIMIT = 48 * 1024 * 1024


def dot(a, b):
    return jnp.dot(a, b, precision=HI, preferred_element_type=jnp.float32)


def dot_dims(a, b, da, db):
    return lax.dot_general(
        a, b, (((da,), (db,)), ((), ())), precision=HI, preferred_element_type=jnp.float32
    )


def wide(x):
    return jnp.broadcast_to(x, (SUB, LANES))


def lower_blocks(n):
    return [(i, j) for i in range(n) for j in range(i + 1)]


def call(kernel, out_shape, specs, scratch=(), flops=0, name=None, limit=LIMIT):
    return pl.pallas_call(
        kernel,
        out_shape=out_shape,
        in_specs=specs,
        out_specs=jax.tree.map(lambda _: VMEM, out_shape),
        scratch_shapes=list(scratch),
        compiler_params=pltpu.CompilerParams(vmem_limit_bytes=limit),
        cost_estimate=pl.CostEstimate(flops=flops, bytes_accessed=1 << 20, transcendentals=0),
        name=name,
    )


def shape(*dims):
    return jax.ShapeDtypeStruct(dims, jnp.float32)


def operator(cells_ref, weights_ref, batch, start, count):
    foot, obs = cells_ref.shape[1], cells_ref.shape[2]
    positions = start + lax.broadcasted_iota(jnp.int32, (count, obs), 0)
    total = jnp.zeros((count, obs), jnp.float32)
    for f in range(foot):
        hit = cells_ref[batch, f:f + 1, :] == positions
        total = total + jnp.where(hit, weights_ref[batch, f:f + 1, :], 0.0)
    return total


def project_kernel(
    at_ref, cov_in, mean_in, cells_in, weights_in, send_ref, c_ref, s_ref, cov_ref, mean_ref, cells_ref, weights_ref, sems
):
    moves = [
        pltpu.make_async_copy(src, dst, sems.at[n])
        for n, (src, dst) in enumerate(
            [(cells_in, cells_ref), (weights_in, weights_ref), (cov_in, cov_ref), (mean_in, mean_ref)]
        )
    ]
    for move in moves:
        move.start()
    for move in moves:
        move.wait()
    rows, cols = cov_ref.shape
    batches, _, obs = cells_ref.shape
    plane = send_ref.shape[0]
    nb = batches * obs // LANES
    per = obs // LANES
    row_ops = []
    cov = cov_ref[...]
    for b in range(batches):
        col_op = operator(cells_ref, weights_ref, b, at_ref[1] * cols, cols)
        row_ops.append(operator(cells_ref, weights_ref, b, at_ref[0] * rows, rows))
        c_ref[:, b * obs:(b + 1) * obs] = dot(cov, col_op)
    for i in range(batches):
        for j in range(i + 1):
            s_ref[i * obs:(i + 1) * obs, j * obs:(j + 1) * obs] = dot_dims(
                row_ops[i], c_ref[:, j * obs:(j + 1) * obs], 0, 0
            )
    low = lower_blocks(nb)
    tiles = len(low) * GROUPS // plane
    lane = lax.broadcasted_iota(jnp.int32, (SUB, LANES), 1)
    sub = lax.broadcasted_iota(jnp.int32, (SUB, LANES), 0)
    mean = jnp.broadcast_to(mean_ref[...], (SUB, rows))
    mean = jnp.where(at_ref[1] == 0, mean, 0.0)
    preds = [dot(mean, row_ops[b]) for b in range(batches)]
    for n, (i, j) in enumerate(low):
        for g in range(GROUPS):
            t = s_ref[i * LANES + g * SUB:i * LANES + (g + 1) * SUB, j * LANES:(j + 1) * LANES]
            if i == j and g == 0:
                p = preds[i // per][:, (i % per) * LANES:(i % per + 1) * LANES]
                t = jnp.where((sub == 0) & (lane > 0), p, t)
                t = jnp.where((sub == 1) & (lane == LANES - 1), wide(p[:, :1]), t)
            q = n * GROUPS + g
            send_ref[q // tiles, (q % tiles) * SUB:(q % tiles + 1) * SUB, :] = t
    own = rows // plane
    for i in range(plane):
        for j in range(nb):
            at = (tiles + j) * SUB
            send_ref[i, at:at + own, :] = c_ref[i * own:(i + 1) * own, j * LANES:(j + 1) * LANES]


def inverse_factor(v, jobs):
    v = list(v)
    lane = lax.broadcasted_iota(jnp.int32, (SUB, LANES), 1)
    sub = lax.broadcasted_iota(jnp.int32, (SUB, LANES), 0)
    out = []
    following = None
    for p in range(len(v)):
        last = p + 1 == len(v)
        t = v[p]
        base = p * SUB
        inside = (lane >= base) & (lane < base + SUB)
        col = following or [wide(t[:, base + s:base + s + 1]) for s in range(SUB)]
        ahead, square = [], []
        if not last:
            nxt = base + SUB
            ahead = [wide(t[:, nxt + s:nxt + s + 1]) for s in range(SUB)]
            square = [wide(v[p + 1][:, nxt + s:nxt + s + 1]) for s in range(SUB)]
        t = jnp.where(inside, jnp.where(lane - base == sub, 1.0, 0.0), t)
        low = t
        piv = jnp.ones((SUB, LANES), jnp.float32)
        pairs = []
        for u in range(0, SUB, 2):
            a = wide(col[u][u:u + 1])
            b = wide(col[u + 1][u:u + 1])
            c = wide(col[u + 1][u + 1:u + 2])
            det = a * c - b * b
            rd = pltpu.reciprocal(det, approx=True)
            ra = pltpu.reciprocal(a, approx=True)
            here = (sub == u) | (sub == u + 1)
            c1 = jnp.where(here, 0.0, col[u])
            c2 = jnp.where(here, 0.0, col[u + 1])
            m1 = (c1 * c - c2 * b) * rd
            m2 = (c2 * a - c1 * b) * rd

            def clear(z):
                return z - (m1 * wide(z[u:u + 1]) + m2 * wide(z[u + 1:u + 2]))

            for w in range(u + 2, SUB):
                col[w] = clear(col[w])
            ahead = [clear(z) for z in ahead]
            t = clear(t)
            low = jnp.where(
                sub > u + 1, clear(low), jnp.where(sub == u + 1, low - (b * ra) * wide(low[u:u + 1]), low)
            )
            piv = jnp.where(sub == u, a, jnp.where(sub == u + 1, det * ra, piv))
            pairs.append((a * rd, b * rd, c * rd))
        out.append(jnp.where(lane <= sub + base, low * lax.rsqrt(piv), 0.0))

        def solved(z):
            q = []
            for u in range(0, SUB, 2):
                ar, br, cr = pairs[u // 2]
                z0, z1 = wide(z[u:u + 1]), wide(z[u + 1:u + 2])
                q.extend((z0 * cr - z1 * br, z1 * ar - z0 * br))
            return q

        def less(w, c, q):
            g = [c[s] * q[s] for s in range(SUB)]
            return w - (((g[0] + g[1]) + (g[2] + g[3])) + ((g[4] + g[5]) + (g[6] + g[7])))

        if not last:
            q = solved(t)
            following = None
            for j in range(p + 1, len(v)):
                c = [wide(v[j][:, base + s:base + s + 1]) for s in range(SUB)]
                v[j] = less(jnp.where(inside, 0.0, v[j]), c, q)
                if following is None:
                    following = [less(square[s], c, solved(ahead[s])) for s in range(SUB)]
        if jobs:
            jobs.pop(0)()
    while jobs:
        jobs.pop(0)()
    return jnp.concatenate(out, axis=0)


def factor_kernel(
    got_ref, values_ref, variance_ref, mean_ref, linv_ref, gain_ref, after_ref, a_ref, l_ref, e_ref, y_ref
):
    nb = values_ref.shape[0]
    rows = gain_ref.shape[0]
    low = lower_blocks(nb)
    plane = got_ref.shape[0]
    tiles = len(low) * GROUPS // plane
    own = rows // plane
    for n, (i, j) in enumerate(low):
        for g in range(GROUPS):
            q = n * GROUPS + g
            a_ref[i, j, g * SUB:(g + 1) * SUB, :] = got_ref[
                q // tiles, (q % tiles) * SUB:(q % tiles + 1) * SUB, :
            ]
    for i in range(plane):
        for j in range(nb):
            at = tiles * SUB + j * own
            e_ref[j, i * own:(i + 1) * own, :] = got_ref[i, at:at + own, :]
    r_io = lax.broadcasted_iota(jnp.int32, (LANES, LANES), 0)
    l_io = lax.broadcasted_iota(jnp.int32, (LANES, LANES), 1)
    lane = lax.broadcasted_iota(jnp.int32, (SUB, LANES), 1)
    for i in range(nb):
        first = a_ref[i, i, 0:SUB, :]
        pred = jnp.where(lane == 0, wide(first[1:2, LANES - 1:LANES]), wide(first[0:1, :]))
        e_ref[i, rows:rows + SUB, :] = wide(values_ref[i:i + 1, :]) - pred
        d = a_ref[i, i]
        below = jnp.where(r_io > l_io, d, 0.0)
        diag = jnp.where(r_io == l_io, d + variance_ref[i:i + 1, :], 0.0)
        a_ref[i, i] = below + below.T + diag
    for i in range(nb):
        for j in range(i + 1, nb):
            linv_ref[i * LANES:(i + 1) * LANES, j * LANES:(j + 1) * LANES] = jnp.zeros(
                (LANES, LANES), jnp.float32
            )

    def span(i):
        return slice(i * LANES, (i + 1) * LANES)

    def scale(j, i, x):
        l_ref[j, i] = dot_dims(a_ref[j, i], x, 1, 1)

    def reduce(j, k, i):
        a_ref[j, k] = a_ref[j, k] - dot_dims(l_ref[j, i], l_ref[k, i], 1, 1)

    def scale_rows(i, x):
        e_ref[i] = dot_dims(e_ref[i], x, 1, 1)

    def reduce_rows(k, i):
        e_ref[k] = e_ref[k] - dot_dims(e_ref[i], l_ref[k, i], 1, 1)

    def gather(i):
        acc = dot(l_ref[i, 0], linv_ref[0:LANES, 0:i * LANES])
        for k in range(1, i):
            acc = acc + dot(l_ref[i, k], linv_ref[span(k), 0:i * LANES])
        y_ref[:, 0:i * LANES] = acc

    def finish(i):
        linv_ref[span(i), 0:i * LANES] = -dot(linv_ref[span(i), span(i)], y_ref[:, 0:i * LANES])

    def work(f, *args):
        return lambda: f(*args)

    jobs = []
    for i in range(nb):
        x = inverse_factor([a_ref[i, i, g * SUB:(g + 1) * SUB, :] for g in range(GROUPS)], jobs)
        linv_ref[span(i), span(i)] = x
        if i + 1 < nb:
            scale(i + 1, i, x)
            reduce(i + 1, i + 1, i)
            for j in range(i + 2, nb):
                jobs.append(work(scale, j, i, x))
            for k in range(i + 1, nb):
                for j in range(max(k, i + 2), nb):
                    jobs.append(work(reduce, j, k, i))
            jobs.append(work(scale_rows, i, x))
            for k in range(i + 1, nb):
                jobs.append(work(reduce_rows, k, i))
            if i > 0:
                jobs.append(work(finish, i))
            jobs.append(work(gather, i + 1))
        else:
            scale_rows(i, x)
            finish(i)
    for i in range(nb):
        gain_ref[:, span(i)] = e_ref[i, 0:rows, :]
    after = jnp.broadcast_to(mean_ref[...], (SUB, rows))
    for i in range(nb):
        after = after + dot_dims(e_ref[i, rows:rows + SUB, :], e_ref[i, 0:rows, :], 1, 1)
    after_ref[...] = after[0:1]


def update_kernel(cov_ref, pieces_ref, linv_ref, gain_ref, out_ref, c_ref):
    n_row, halves, tall, _ = pieces_ref.shape
    cols, m = c_ref.shape
    nb = m // LANES
    own = tall // nb
    for h in range(halves):
        for r in range(n_row):
            z, k = divmod(r, 2)
            at = h * (cols // halves) + (k * (n_row // 2) + z) * own
            for j in range(nb):
                c_ref[at:at + own, j * LANES:(j + 1) * LANES] = pieces_ref[r, h, j * own:(j + 1) * own, :]
    gain_cols = dot_dims(c_ref[...], linv_ref[...], 1, 1)
    out_ref[...] = cov_ref[...] - dot_dims(gain_ref[...], gain_cols, 1, 1)


def on_device(covariance, state_mean, obs_values, obs_cells, obs_weights, obs_variance):
    rows, cols = covariance.shape
    n_row, n_col = lax.axis_size("row"), lax.axis_size("col")
    n_z = n_row // 2
    row, col = lax.axis_index("row"), lax.axis_index("col")
    plane = 2 * n_col
    batches, _, obs = obs_cells.shape
    m = batches * obs
    nb = m // LANES
    own = rows // plane
    c_rows = own * nb
    s_rows = nb * (nb + 1) // 2 * LANES // plane
    chunk = s_rows + c_rows
    at = jnp.stack([row, col]).astype(jnp.int32)
    mean = state_mean.reshape(1, rows)

    plane_groups = [[z * plane + i for i in range(plane)] for z in range(n_z)]
    z_groups = [[2 * z + k for z in range(n_z)] for k in range(2)]
    pairs = []
    for idx in range(n_row * n_col):
        r, c = divmod(idx, n_col)
        z, k = divmod(r, 2)
        pairs.append((idx, (2 * c + k) * n_col + z))

    send = call(
        project_kernel,
        shape(plane, chunk, LANES),
        [SMEM] + [HBM] * 4,
        [
            pltpu.VMEM((rows, m), jnp.float32),
            pltpu.VMEM((m, m), jnp.float32),
            pltpu.VMEM((rows, cols), jnp.float32),
            pltpu.VMEM((1, rows), jnp.float32),
            pltpu.VMEM(obs_cells.shape, jnp.int32),
            pltpu.VMEM(obs_weights.shape, jnp.float32),
            pltpu.SemaphoreType.DMA((4,)),
        ],
        flops=2 * rows * m * (cols + m),
        name="project",
        limit=60 * 1024 * 1024,
    )(at, covariance, mean, obs_cells, obs_weights)
    got = lax.all_to_all(send, ("row", "col"), 0, 0, axis_index_groups=plane_groups)
    s_chunk = jnp.sum(got[:, :s_rows], axis=0)
    c_own = jnp.sum(got[:, s_rows:].reshape(2, n_col, c_rows, LANES), axis=1)

    s_send = jnp.broadcast_to(s_chunk[None], (n_z, s_rows, LANES))
    c_tr = lax.ppermute(c_own, ("row", "col"), pairs)
    s_send, c_tr = lax.optimization_barrier((s_send, c_tr))
    s_all = lax.all_to_all(s_send, "row", 0, 0, axis_index_groups=z_groups)
    c_cols = lax.all_gather(c_tr, "row")
    s_full = jnp.sum(s_all, axis=0)
    send2 = jnp.concatenate(
        [
            jnp.broadcast_to(s_full[None], (plane, s_rows, LANES)),
            jnp.broadcast_to(c_own[:, None], (2, n_col, c_rows, LANES)).reshape(plane, c_rows, LANES),
        ],
        axis=1,
    )
    got2 = lax.all_to_all(send2, ("row", "col"), 0, 0, axis_index_groups=plane_groups)
    linv, gain, after = call(
        factor_kernel,
        (shape(m, m), shape(rows, m), shape(1, rows)),
        [VMEM] * 4,
        [
            pltpu.VMEM((nb, nb, LANES, LANES), jnp.float32),
            pltpu.VMEM((nb, nb, LANES, LANES), jnp.float32),
            pltpu.VMEM((nb, rows + SUB, LANES), jnp.float32),
            pltpu.VMEM((LANES, m), jnp.float32),
        ],
        flops=1 << 20,
        name="factor",
    )(got2, obs_values.reshape(nb, LANES), obs_variance.reshape(nb, LANES), mean)
    updated = call(
        update_kernel,
        shape(rows, cols),
        [VMEM] * 4,
        [pltpu.VMEM((cols, m), jnp.float32)],
        flops=1 << 31,
        name="update",
    )(covariance, c_cols, linv, gain)
    return (updated, after.reshape(rows))


def solution(mesh):
    return jax.shard_map(
        on_device,
        mesh=mesh,
        in_specs=(P("row", "col"), P("row"), P(), P(), P(), P()),
        out_specs=(P("row", "col"), P("row")),
        check_vma=False,
    )
```

```python
import jax
import jax.numpy as jnp
from jax import lax
from jax.experimental import pallas as pl
from jax.experimental.pallas import tpu as pltpu
from jax.sharding import PartitionSpec as P

SUB = 8
LANES = 128
GROUPS = LANES // SUB
HI = lax.Precision.HIGHEST
HBM = pl.BlockSpec(memory_space=pltpu.HBM)
VMEM = pl.BlockSpec(memory_space=pltpu.VMEM)
SMEM = pl.BlockSpec(memory_space=pltpu.SMEM)
LIMIT = 48 * 1024 * 1024


def dot(a, b):
    return jnp.dot(a, b, precision=HI, preferred_element_type=jnp.float32)


def dot_dims(a, b, da, db):
    return lax.dot_general(
        a, b, (((da,), (db,)), ((), ())), precision=HI, preferred_element_type=jnp.float32
    )


def wide(x):
    return jnp.broadcast_to(x, (SUB, LANES))


def lower_blocks(n):
    return [(i, j) for i in range(n) for j in range(i + 1)]


def call(kernel, out_shape, specs, scratch=(), flops=0, name=None, aliases=None, limit=LIMIT):
    return pl.pallas_call(
        kernel,
        out_shape=out_shape,
        in_specs=specs,
        out_specs=jax.tree.map(lambda _: VMEM, out_shape),
        scratch_shapes=list(scratch),
        input_output_aliases=aliases or {},
        compiler_params=pltpu.CompilerParams(vmem_limit_bytes=limit),
        cost_estimate=pl.CostEstimate(flops=flops, bytes_accessed=1 << 20, transcendentals=0),
        name=name,
    )


def shape(*dims):
    return jax.ShapeDtypeStruct(dims, jnp.float32)


def operator(cells_ref, weights_ref, batch, start, count):
    foot, obs = cells_ref.shape[1], cells_ref.shape[2]
    positions = start + lax.broadcasted_iota(jnp.int32, (count, obs), 0)
    total = jnp.zeros((count, obs), jnp.float32)
    for f in range(foot):
        hit = cells_ref[batch, f:f + 1, :] == positions
        total = total + jnp.where(hit, weights_ref[batch, f:f + 1, :], 0.0)
    return total


def project_kernel(
    at_ref, cov_in, mean_in, cells_in, weights_in, send_ref, c_ref, s_ref, cov_ref, mean_ref, cells_ref, weights_ref, sems
):
    moves = [
        pltpu.make_async_copy(src, dst, sems.at[n])
        for n, (src, dst) in enumerate(
            [(cells_in, cells_ref), (weights_in, weights_ref), (cov_in, cov_ref), (mean_in, mean_ref)]
        )
    ]
    for move in moves:
        move.start()
    for move in moves:
        move.wait()
    rows, cols = cov_ref.shape
    batches, _, obs = cells_ref.shape
    plane = send_ref.shape[0]
    nb = batches * obs // LANES
    per = obs // LANES
    row_ops = []
    cov = cov_ref[...]
    for b in range(batches):
        col_op = operator(cells_ref, weights_ref, b, at_ref[1] * cols, cols)
        row_ops.append(operator(cells_ref, weights_ref, b, at_ref[0] * rows, rows))
        c_ref[:, b * obs:(b + 1) * obs] = dot(cov, col_op)
    for i in range(batches):
        for j in range(i + 1):
            s_ref[i * obs:(i + 1) * obs, j * obs:(j + 1) * obs] = dot_dims(
                row_ops[i], c_ref[:, j * obs:(j + 1) * obs], 0, 0
            )
    low = lower_blocks(nb)
    tiles = len(low) * GROUPS // plane
    lane = lax.broadcasted_iota(jnp.int32, (SUB, LANES), 1)
    sub = lax.broadcasted_iota(jnp.int32, (SUB, LANES), 0)
    mean = jnp.broadcast_to(mean_ref[...], (SUB, rows))
    mean = jnp.where(at_ref[1] == 0, mean, 0.0)
    preds = [dot(mean, row_ops[b]) for b in range(batches)]
    for n, (i, j) in enumerate(low):
        for g in range(GROUPS):
            t = s_ref[i * LANES + g * SUB:i * LANES + (g + 1) * SUB, j * LANES:(j + 1) * LANES]
            if i == j and g == 0:
                p = preds[i // per][:, (i % per) * LANES:(i % per + 1) * LANES]
                t = jnp.where((sub == 0) & (lane > 0), p, t)
                t = jnp.where((sub == 1) & (lane == LANES - 1), wide(p[:, :1]), t)
            q = n * GROUPS + g
            send_ref[q // tiles, (q % tiles) * SUB:(q % tiles + 1) * SUB, :] = t
    own = rows // plane
    for i in range(plane):
        for j in range(nb):
            at = (tiles + j) * SUB
            send_ref[i, at:at + own, :] = c_ref[i * own:(i + 1) * own, j * LANES:(j + 1) * LANES]


def inverse_factor(v, jobs):
    v = list(v)
    lane = lax.broadcasted_iota(jnp.int32, (SUB, LANES), 1)
    sub = lax.broadcasted_iota(jnp.int32, (SUB, LANES), 0)
    out = []
    following = None
    for p in range(len(v)):
        last = p + 1 == len(v)
        t = v[p]
        base = p * SUB
        inside = (lane >= base) & (lane < base + SUB)
        col = following or [wide(t[:, base + s:base + s + 1]) for s in range(SUB)]
        ahead, square = [], []
        if not last:
            nxt = base + SUB
            ahead = [wide(t[:, nxt + s:nxt + s + 1]) for s in range(SUB)]
            square = [wide(v[p + 1][:, nxt + s:nxt + s + 1]) for s in range(SUB)]
        t = jnp.where(inside, jnp.where(lane - base == sub, 1.0, 0.0), t)
        low = t
        piv = jnp.ones((SUB, LANES), jnp.float32)
        pairs = []
        for u in range(0, SUB, 2):
            a = wide(col[u][u:u + 1])
            b = wide(col[u + 1][u:u + 1])
            c = wide(col[u + 1][u + 1:u + 2])
            det = a * c - b * b
            rd = pltpu.reciprocal(det, approx=True)
            ra = pltpu.reciprocal(a, approx=True)
            here = (sub == u) | (sub == u + 1)
            c1 = jnp.where(here, 0.0, col[u])
            c2 = jnp.where(here, 0.0, col[u + 1])
            m1 = (c1 * c - c2 * b) * rd
            m2 = (c2 * a - c1 * b) * rd

            def clear(z):
                return z - (m1 * wide(z[u:u + 1]) + m2 * wide(z[u + 1:u + 2]))

            for w in range(u + 2, SUB):
                col[w] = clear(col[w])
            ahead = [clear(z) for z in ahead]
            t = clear(t)
            low = jnp.where(
                sub > u + 1, clear(low), jnp.where(sub == u + 1, low - (b * ra) * wide(low[u:u + 1]), low)
            )
            piv = jnp.where(sub == u, a, jnp.where(sub == u + 1, det * ra, piv))
            pairs.append((a * rd, b * rd, c * rd))
        out.append(jnp.where(lane <= sub + base, low * lax.rsqrt(piv), 0.0))

        def solved(z):
            q = []
            for u in range(0, SUB, 2):
                ar, br, cr = pairs[u // 2]
                z0, z1 = wide(z[u:u + 1]), wide(z[u + 1:u + 2])
                q.extend((z0 * cr - z1 * br, z1 * ar - z0 * br))
            return q

        def less(w, c, q):
            g = [c[s] * q[s] for s in range(SUB)]
            return w - (((g[0] + g[1]) + (g[2] + g[3])) + ((g[4] + g[5]) + (g[6] + g[7])))

        if not last:
            q = solved(t)
            following = None
            for j in range(p + 1, len(v)):
                c = [wide(v[j][:, base + s:base + s + 1]) for s in range(SUB)]
                v[j] = less(jnp.where(inside, 0.0, v[j]), c, q)
                if following is None:
                    following = [less(square[s], c, solved(ahead[s])) for s in range(SUB)]
        if jobs:
            jobs.pop(0)()
    while jobs:
        jobs.pop(0)()
    return jnp.concatenate(out, axis=0)


def prepare(got_ref, values_ref, variance_ref, linv_ref, a_ref, e_ref):
    nb = values_ref.shape[0]
    rows = e_ref.shape[1] - SUB
    low = lower_blocks(nb)
    plane = got_ref.shape[0]
    tiles = len(low) * GROUPS // plane
    own = rows // plane
    for n, (i, j) in enumerate(low):
        for g in range(GROUPS):
            q = n * GROUPS + g
            a_ref[i, j, g * SUB:(g + 1) * SUB, :] = got_ref[
                q // tiles, (q % tiles) * SUB:(q % tiles + 1) * SUB, :
            ]
    for i in range(plane):
        for j in range(nb):
            at = tiles * SUB + j * own
            e_ref[j, i * own:(i + 1) * own, :] = got_ref[i, at:at + own, :]
    r_io = lax.broadcasted_iota(jnp.int32, (LANES, LANES), 0)
    l_io = lax.broadcasted_iota(jnp.int32, (LANES, LANES), 1)
    lane = lax.broadcasted_iota(jnp.int32, (SUB, LANES), 1)
    for i in range(nb):
        first = a_ref[i, i, 0:SUB, :]
        pred = jnp.where(lane == 0, wide(first[1:2, LANES - 1:LANES]), wide(first[0:1, :]))
        e_ref[i, rows:rows + SUB, :] = wide(values_ref[i:i + 1, :]) - pred
        d = a_ref[i, i]
        below = jnp.where(r_io > l_io, d, 0.0)
        diag = jnp.where(r_io == l_io, d + variance_ref[i:i + 1, :], 0.0)
        a_ref[i, i] = below + below.T + diag
    for i in range(nb):
        for j in range(i + 1, nb):
            linv_ref[i * LANES:(i + 1) * LANES, j * LANES:(j + 1) * LANES] = jnp.zeros(
                (LANES, LANES), jnp.float32
            )


def factor_steps(begin, end, linv_ref, a_ref, l_ref, e_ref, y_ref):
    nb = a_ref.shape[0]

    def span(i):
        return slice(i * LANES, (i + 1) * LANES)

    def scale(j, i):
        l_ref[j, i] = dot_dims(a_ref[j, i], linv_ref[span(i), span(i)], 1, 1)

    def reduce(j, k, i):
        a_ref[j, k] = a_ref[j, k] - dot_dims(l_ref[j, i], l_ref[k, i], 1, 1)

    def scale_rows(i):
        e_ref[i] = dot_dims(e_ref[i], linv_ref[span(i), span(i)], 1, 1)

    def reduce_rows(k, i):
        e_ref[k] = e_ref[k] - dot_dims(e_ref[i], l_ref[k, i], 1, 1)

    def gather(i):
        acc = dot(l_ref[i, 0], linv_ref[0:LANES, 0:i * LANES])
        for k in range(1, i):
            acc = acc + dot(l_ref[i, k], linv_ref[span(k), 0:i * LANES])
        y_ref[:, 0:i * LANES] = acc

    def finish(i):
        linv_ref[span(i), 0:i * LANES] = -dot(linv_ref[span(i), span(i)], y_ref[:, 0:i * LANES])

    def work(f, *args):
        return lambda: f(*args)

    def rest(i):
        todo = [work(scale, j, i) for j in range(i + 2, nb)]
        todo += [work(reduce, j, k, i) for k in range(i + 1, nb) for j in range(max(k, i + 2), nb)]
        todo.append(work(scale_rows, i))
        todo += [work(reduce_rows, k, i) for k in range(i + 1, nb)]
        if i > 0:
            todo.append(work(finish, i))
        todo.append(work(gather, i + 1))
        return todo

    for i in range(begin, end):
        jobs = rest(i - 1) if i > 0 else []
        linv_ref[span(i), span(i)] = inverse_factor(
            [a_ref[i, i, g * SUB:(g + 1) * SUB, :] for g in range(GROUPS)], jobs
        )
        if i + 1 < nb:
            scale(i + 1, i)
            reduce(i + 1, i + 1, i)
        else:
            scale_rows(i)
            finish(i)


def early_kernel(got_ref, values_ref, variance_ref, linv_ref, a_ref, l_ref, e_ref, y_ref):
    prepare(got_ref, values_ref, variance_ref, linv_ref, a_ref, e_ref)
    factor_steps(0, a_ref.shape[0] - 2, linv_ref, a_ref, l_ref, e_ref, y_ref)


def middle_kernel(linv_in, a_in, l_in, e_in, y_in, linv_ref, a_ref, l_ref, e_ref, y_ref):
    nb = a_ref.shape[0]
    factor_steps(nb - 2, nb - 1, linv_ref, a_ref, l_ref, e_ref, y_ref)


def late_kernel(
    mean_ref, linv_in, a_in, l_in, e_in, y_in, linv_ref, a_ref, l_ref, e_ref, y_ref, after_ref
):
    nb = a_ref.shape[0]
    rows = e_ref.shape[1] - SUB
    factor_steps(nb - 1, nb, linv_ref, a_ref, l_ref, e_ref, y_ref)
    after = jnp.broadcast_to(mean_ref[...], (SUB, rows))
    for i in range(nb):
        after = after + dot_dims(e_ref[i, rows:rows + SUB, :], e_ref[i, 0:rows, :], 1, 1)
    after_ref[...] = after[0:1]


def update_kernel(at_ref, cov_ref, mine_ref, other_ref, linv_ref, e_ref, out_ref, c_ref):
    n_z, halves, tall, _ = mine_ref.shape
    rows, cols = cov_ref.shape
    m = c_ref.shape[1]
    nb = m // LANES
    own = tall // nb
    core = lax.rem(at_ref[0], 2)
    z_here = lax.div(at_ref[0], 2)
    for ref, k in ((mine_ref, core), (other_ref, 1 - core)):
        for d in range(n_z):
            start = pl.multiple_of((k * n_z + lax.bitwise_xor(z_here, d)) * own, own)
            for h in range(halves):
                for j in range(nb):
                    c_ref[pl.ds(start + h * (cols // halves), own), j * LANES:(j + 1) * LANES] = ref[
                        d, h, j * own:(j + 1) * own, :
                    ]
    gain_cols = dot_dims(c_ref[...], linv_ref[...], 1, 1)
    gain = jnp.concatenate([e_ref[j, 0:rows, :] for j in range(nb)], axis=1)
    out_ref[...] = cov_ref[...] - dot_dims(gain, gain_cols, 1, 1)


def on_device(covariance, state_mean, obs_values, obs_cells, obs_weights, obs_variance):
    rows, cols = covariance.shape
    n_row, n_col = lax.axis_size("row"), lax.axis_size("col")
    n_z = n_row // 2
    row, col = lax.axis_index("row"), lax.axis_index("col")
    plane = 2 * n_col
    batches, _, obs = obs_cells.shape
    m = batches * obs
    nb = m // LANES
    own = rows // plane
    c_rows = own * nb
    s_rows = nb * (nb + 1) // 2 * LANES // plane
    chunk = s_rows + c_rows
    at = jnp.stack([row, col]).astype(jnp.int32)
    mean = state_mean.reshape(1, rows)

    plane_groups = [[z * plane + i for i in range(plane)] for z in range(n_z)]
    z_groups = [[2 * z + k for z in range(n_z)] for k in range(2)]
    pairs = []
    for idx in range(n_row * n_col):
        r, c = divmod(idx, n_col)
        z, k = divmod(r, 2)
        pairs.append((idx, (2 * c + k) * n_col + z))

    send = call(
        project_kernel,
        shape(plane, chunk, LANES),
        [SMEM] + [HBM] * 4,
        [
            pltpu.VMEM((rows, m), jnp.float32),
            pltpu.VMEM((m, m), jnp.float32),
            pltpu.VMEM((rows, cols), jnp.float32),
            pltpu.VMEM((1, rows), jnp.float32),
            pltpu.VMEM(obs_cells.shape, jnp.int32),
            pltpu.VMEM(obs_weights.shape, jnp.float32),
            pltpu.SemaphoreType.DMA((4,)),
        ],
        flops=2 * rows * m * (cols + m),
        name="project",
        limit=60 * 1024 * 1024,
    )(at, covariance, mean, obs_cells, obs_weights)
    got = lax.all_to_all(send, ("row", "col"), 0, 0, axis_index_groups=plane_groups)
    s_chunk = jnp.sum(got[:, :s_rows], axis=0)
    c_own = jnp.sum(got[:, s_rows:].reshape(2, n_col, c_rows, LANES), axis=1)

    s_send = jnp.broadcast_to(s_chunk[None], (n_z, s_rows, LANES))
    c_tr = lax.ppermute(c_own, ("row", "col"), pairs)
    s_all = lax.all_to_all(s_send, "row", 0, 0, axis_index_groups=z_groups)
    s_full = jnp.sum(s_all, axis=0)
    send2 = jnp.concatenate(
        [
            jnp.broadcast_to(s_full[None], (plane, s_rows, LANES)),
            jnp.broadcast_to(c_own[:, None], (2, n_col, c_rows, LANES)).reshape(plane, c_rows, LANES),
        ],
        axis=1,
    )
    send2, c_tr = lax.optimization_barrier((send2, c_tr))
    got2 = lax.all_to_all(send2, ("row", "col"), 0, 0, axis_index_groups=plane_groups)

    def partner(x, bit):
        return lax.ppermute(x, "row", [(i, i ^ bit) for i in range(n_row)])

    pieces = c_tr[None]
    bits = []
    while 1 << len(bits) < n_z:
        bits.append(2 << len(bits))
    def doubled(x, theirs):
        return jnp.concatenate([x[:, None], theirs[:, None]], axis=1).reshape((-1,) + c_tr.shape)

    for bit in bits[:1:-1]:
        pieces = doubled(pieces, partner(pieces, bit))
    got2, pieces = lax.optimization_barrier((got2, pieces))
    state = (
        shape(m, m),
        shape(nb, nb, LANES, LANES),
        shape(nb, nb, LANES, LANES),
        shape(nb, rows + SUB, LANES),
        shape(LANES, m),
    )
    theirs = partner(pieces, bits[1])
    held = call(early_kernel, state, [VMEM] * 3, flops=1 << 30, name="early")(
        got2, obs_values.reshape(nb, LANES), obs_variance.reshape(nb, LANES)
    )
    held, theirs = lax.optimization_barrier((held, theirs))
    pieces = doubled(pieces, theirs)
    theirs = partner(pieces, bits[0])
    held = call(
        middle_kernel,
        state,
        [VMEM] * 5,
        flops=1 << 30,
        name="middle",
        aliases={n: n for n in range(len(state))},
    )(*held)
    held, theirs = lax.optimization_barrier((held, theirs))
    pieces = doubled(pieces, theirs)
    other = partner(pieces, 1)
    out = call(
        late_kernel,
        state + (shape(1, rows),),
        [VMEM] * 6,
        flops=1 << 30,
        name="late",
        aliases={n + 1: n for n in range(len(state))},
    )(mean, *held)
    linv, e, after = out[0], out[3], out[5]
    updated = call(
        update_kernel,
        shape(rows, cols),
        [SMEM] + [VMEM] * 5,
        [pltpu.VMEM((cols, m), jnp.float32)],
        flops=1 << 31,
        name="update",
    )(at, covariance, pieces, other, linv, e)
    return (updated, after.reshape(rows))


def solution(mesh):
    return jax.shard_map(
        on_device,
        mesh=mesh,
        in_specs=(P("row", "col"), P("row"), P(), P(), P(), P()),
        out_specs=(P("row", "col"), P("row")),
        check_vma=False,
    )
```

```python
import jax
import jax.numpy as jnp
from jax import lax
from jax.experimental import pallas as pl
from jax.experimental.pallas import tpu as pltpu
from jax.sharding import PartitionSpec as P

SUB = 8
LANES = 128
GROUPS = LANES // SUB
HI = lax.Precision.HIGHEST
HBM = pl.BlockSpec(memory_space=pltpu.HBM)
VMEM = pl.BlockSpec(memory_space=pltpu.VMEM)
LIMIT = 48 * 1024 * 1024


def dot(a, b):
    return jnp.dot(a, b, precision=HI, preferred_element_type=jnp.float32)


def dot_dims(a, b, da, db):
    return lax.dot_general(
        a, b, (((da,), (db,)), ((), ())), precision=HI, preferred_element_type=jnp.float32
    )


def wide(x):
    return jnp.broadcast_to(x, (SUB, LANES))


def lower_blocks(n):
    return [(i, j) for i in range(n) for j in range(i + 1)]


def call(kernel, out_shape, specs, scratch=(), flops=0, name=None, aliases=None, limit=LIMIT):
    return pl.pallas_call(
        kernel,
        out_shape=out_shape,
        in_specs=specs,
        out_specs=jax.tree.map(lambda _: VMEM, out_shape),
        scratch_shapes=list(scratch),
        input_output_aliases=aliases or {},
        compiler_params=pltpu.CompilerParams(vmem_limit_bytes=limit),
        cost_estimate=pl.CostEstimate(flops=flops, bytes_accessed=1 << 20, transcendentals=0),
        name=name,
    )


def shape(*dims):
    return jax.ShapeDtypeStruct(dims, jnp.float32)


def operator(cells_ref, weights_ref, batch, start, count):
    foot, obs = cells_ref.shape[1], cells_ref.shape[2]
    positions = start + lax.broadcasted_iota(jnp.int32, (count, obs), 0)
    total = jnp.zeros((count, obs), jnp.float32)
    for f in range(foot):
        hit = cells_ref[batch, f:f + 1, :] == positions
        total = total + jnp.where(hit, weights_ref[batch, f:f + 1, :], 0.0)
    return total


def project_kernel(
    cov_in, mean_in, cells_in, weights_in, send_ref, c_ref, s_ref, cov_ref, mean_ref, cells_ref, weights_ref, sems
):
    moves = [
        pltpu.make_async_copy(src, dst, sems.at[n])
        for n, (src, dst) in enumerate(
            [(cells_in, cells_ref), (weights_in, weights_ref), (cov_in, cov_ref), (mean_in, mean_ref)]
        )
    ]
    for move in moves:
        move.start()
    moves[0].wait()
    moves[1].wait()
    rows, cols = cov_ref.shape
    row, col = lax.axis_index("row"), lax.axis_index("col")
    batches, _, obs = cells_ref.shape
    plane = send_ref.shape[0]
    nb = batches * obs // LANES
    per = obs // LANES
    row_ops = [operator(cells_ref, weights_ref, b, row * rows, rows) for b in range(batches)]
    col_ops = [operator(cells_ref, weights_ref, b, col * cols, cols) for b in range(batches)]
    moves[2].wait()
    moves[3].wait()
    cov = cov_ref[...]
    for b in range(batches):
        c_ref[:, b * obs:(b + 1) * obs] = dot(cov, col_ops[b])
    for i in range(batches):
        for j in range(i + 1):
            s_ref[i * obs:(i + 1) * obs, j * obs:(j + 1) * obs] = dot_dims(
                row_ops[i], c_ref[:, j * obs:(j + 1) * obs], 0, 0
            )
    low = lower_blocks(nb)
    tiles = len(low) * GROUPS // plane
    lane = lax.broadcasted_iota(jnp.int32, (SUB, LANES), 1)
    sub = lax.broadcasted_iota(jnp.int32, (SUB, LANES), 0)
    mean = jnp.broadcast_to(mean_ref[...], (SUB, rows))
    mean = jnp.where(col == 0, mean, 0.0)
    preds = [dot(mean, row_ops[b]) for b in range(batches)]
    for n, (i, j) in enumerate(low):
        for g in range(GROUPS):
            t = s_ref[i * LANES + g * SUB:i * LANES + (g + 1) * SUB, j * LANES:(j + 1) * LANES]
            if i == j and g == 0:
                p = preds[i // per][:, (i % per) * LANES:(i % per + 1) * LANES]
                t = jnp.where((sub == 0) & (lane > 0), p, t)
                t = jnp.where((sub == 1) & (lane == LANES - 1), wide(p[:, :1]), t)
            q = n * GROUPS + g
            send_ref[q // tiles, (q % tiles) * SUB:(q % tiles + 1) * SUB, :] = t
    own = rows // plane
    for i in range(plane):
        for j in range(nb):
            at = (tiles + j) * SUB
            send_ref[i, at:at + own, :] = c_ref[i * own:(i + 1) * own, j * LANES:(j + 1) * LANES]


def inverse_factor(v, jobs):
    v = list(v)
    lane = lax.broadcasted_iota(jnp.int32, (SUB, LANES), 1)
    sub = lax.broadcasted_iota(jnp.int32, (SUB, LANES), 0)
    out = []
    following = None
    for p in range(len(v)):
        last = p + 1 == len(v)
        t = v[p]
        base = p * SUB
        inside = (lane >= base) & (lane < base + SUB)
        col = following or [wide(t[:, base + s:base + s + 1]) for s in range(SUB)]
        ahead, square = [], []
        if not last:
            nxt = base + SUB
            ahead = [wide(t[:, nxt + s:nxt + s + 1]) for s in range(SUB)]
            square = [wide(v[p + 1][:, nxt + s:nxt + s + 1]) for s in range(SUB)]
        t = jnp.where(inside, jnp.where(lane - base == sub, 1.0, 0.0), t)
        low = t
        piv = jnp.ones((SUB, LANES), jnp.float32)
        pairs = []
        for u in range(0, SUB, 2):
            a = wide(col[u][u:u + 1])
            b = wide(col[u + 1][u:u + 1])
            c = wide(col[u + 1][u + 1:u + 2])
            det = a * c - b * b
            rd = pltpu.reciprocal(det, approx=True)
            ra = pltpu.reciprocal(a, approx=True)
            here = (sub == u) | (sub == u + 1)
            c1 = jnp.where(here, 0.0, col[u])
            c2 = jnp.where(here, 0.0, col[u + 1])
            m1 = (c1 * c - c2 * b) * rd
            m2 = (c2 * a - c1 * b) * rd

            def clear(z):
                return z - (m1 * wide(z[u:u + 1]) + m2 * wide(z[u + 1:u + 2]))

            for w in range(u + 2, SUB):
                col[w] = clear(col[w])
            ahead = [clear(z) for z in ahead]
            t = clear(t)
            low = jnp.where(
                sub > u + 1, clear(low), jnp.where(sub == u + 1, low - (b * ra) * wide(low[u:u + 1]), low)
            )
            piv = jnp.where(sub == u, a, jnp.where(sub == u + 1, det * ra, piv))
            pairs.append((a * rd, b * rd, c * rd))
        out.append(jnp.where(lane <= sub + base, low * lax.rsqrt(piv), 0.0))

        def solved(z):
            q = []
            for u in range(0, SUB, 2):
                ar, br, cr = pairs[u // 2]
                z0, z1 = wide(z[u:u + 1]), wide(z[u + 1:u + 2])
                q.extend((z0 * cr - z1 * br, z1 * ar - z0 * br))
            return q

        def less(w, c, q):
            g = [c[s] * q[s] for s in range(SUB)]
            return w - (((g[0] + g[1]) + (g[2] + g[3])) + ((g[4] + g[5]) + (g[6] + g[7])))

        if not last:
            q = solved(t)
            following = None
            for j in range(p + 1, len(v)):
                c = [wide(v[j][:, base + s:base + s + 1]) for s in range(SUB)]
                v[j] = less(jnp.where(inside, 0.0, v[j]), c, q)
                if following is None:
                    following = [less(square[s], c, solved(ahead[s])) for s in range(SUB)]
        if jobs:
            jobs.pop(0)()
    while jobs:
        jobs.pop(0)()
    return jnp.concatenate(out, axis=0)


def prepare(got_ref, values_ref, variance_ref, linv_ref, a_ref, e_ref):
    nb = values_ref.shape[0]
    rows = e_ref.shape[1] - SUB
    low = lower_blocks(nb)
    plane = got_ref.shape[0]
    tiles = len(low) * GROUPS // plane
    own = rows // plane
    for n, (i, j) in enumerate(low):
        for g in range(GROUPS):
            q = n * GROUPS + g
            a_ref[i, j, g * SUB:(g + 1) * SUB, :] = got_ref[
                q // tiles, (q % tiles) * SUB:(q % tiles + 1) * SUB, :
            ]
    for i in range(plane):
        for j in range(nb):
            at = tiles * SUB + j * own
            e_ref[j, i * own:(i + 1) * own, :] = got_ref[i, at:at + own, :]
    r_io = lax.broadcasted_iota(jnp.int32, (LANES, LANES), 0)
    l_io = lax.broadcasted_iota(jnp.int32, (LANES, LANES), 1)
    lane = lax.broadcasted_iota(jnp.int32, (SUB, LANES), 1)
    for i in range(nb):
        first = a_ref[i, i, 0:SUB, :]
        pred = jnp.where(lane == 0, wide(first[1:2, LANES - 1:LANES]), wide(first[0:1, :]))
        e_ref[i, rows:rows + SUB, :] = wide(values_ref[i:i + 1, :]) - pred
        d = a_ref[i, i]
        below = jnp.where(r_io > l_io, d, 0.0)
        diag = jnp.where(r_io == l_io, d + variance_ref[i:i + 1, :], 0.0)
        a_ref[i, i] = below + below.T + diag
    for i in range(nb):
        for j in range(i + 1, nb):
            linv_ref[i * LANES:(i + 1) * LANES, j * LANES:(j + 1) * LANES] = jnp.zeros(
                (LANES, LANES), jnp.float32
            )


def factor_steps(begin, end, linv_ref, a_ref, l_ref, e_ref, y_ref):
    nb = a_ref.shape[0]

    def span(i):
        return slice(i * LANES, (i + 1) * LANES)

    def scale(j, i):
        l_ref[j, i] = dot_dims(a_ref[j, i], linv_ref[span(i), span(i)], 1, 1)

    def reduce(j, k, i):
        a_ref[j, k] = a_ref[j, k] - dot_dims(l_ref[j, i], l_ref[k, i], 1, 1)

    def scale_rows(i):
        e_ref[i] = dot_dims(e_ref[i], linv_ref[span(i), span(i)], 1, 1)

    def reduce_rows(k, i):
        e_ref[k] = e_ref[k] - dot_dims(e_ref[i], l_ref[k, i], 1, 1)

    def gather(i):
        acc = dot(l_ref[i, 0], linv_ref[0:LANES, 0:i * LANES])
        for k in range(1, i):
            acc = acc + dot(l_ref[i, k], linv_ref[span(k), 0:i * LANES])
        y_ref[:, 0:i * LANES] = acc

    def finish(i):
        linv_ref[span(i), 0:i * LANES] = -dot(linv_ref[span(i), span(i)], y_ref[:, 0:i * LANES])

    def work(f, *args):
        return lambda: f(*args)

    def rest(i):
        todo = [work(scale, j, i) for j in range(i + 2, nb)]
        todo += [work(reduce, j, k, i) for k in range(i + 1, nb) for j in range(max(k, i + 2), nb)]
        todo.append(work(scale_rows, i))
        todo += [work(reduce_rows, k, i) for k in range(i + 1, nb)]
        if i > 0:
            todo.append(work(finish, i))
        todo.append(work(gather, i + 1))
        return todo

    for i in range(begin, end):
        jobs = rest(i - 1) if i > 0 else []
        linv_ref[span(i), span(i)] = inverse_factor(
            [a_ref[i, i, g * SUB:(g + 1) * SUB, :] for g in range(GROUPS)], jobs
        )
        if i + 1 < nb:
            scale(i + 1, i)
            reduce(i + 1, i + 1, i)
        else:
            scale_rows(i)
            finish(i)


def early_kernel(got_ref, values_ref, variance_ref, linv_ref, a_ref, l_ref, e_ref, y_ref):
    prepare(got_ref, values_ref, variance_ref, linv_ref, a_ref, e_ref)
    factor_steps(0, a_ref.shape[0] - 1, linv_ref, a_ref, l_ref, e_ref, y_ref)


def late_kernel(
    mean_ref, linv_in, a_in, l_in, e_in, y_in, linv_ref, a_ref, l_ref, e_ref, y_ref, after_ref
):
    nb = a_ref.shape[0]
    rows = e_ref.shape[1] - SUB
    factor_steps(nb - 1, nb, linv_ref, a_ref, l_ref, e_ref, y_ref)
    after = jnp.broadcast_to(mean_ref[...], (SUB, rows))
    for i in range(nb):
        after = after + dot_dims(e_ref[i, rows:rows + SUB, :], e_ref[i, 0:rows, :], 1, 1)
    after_ref[...] = after[0:1]


def update_kernel(cov_ref, mine_ref, other_ref, linv_ref, e_ref, out_ref, c_ref):
    n_z, halves, tall, _ = mine_ref.shape
    rows, cols = cov_ref.shape
    m = c_ref.shape[1]
    nb = m // LANES
    own = tall // nb
    row = lax.axis_index("row")
    core = lax.rem(row, 2)
    z_here = lax.div(row, 2)
    for ref, k in ((mine_ref, core), (other_ref, 1 - core)):
        for d in range(n_z):
            start = pl.multiple_of((k * n_z + lax.bitwise_xor(z_here, d)) * own, own)
            for h in range(halves):
                for j in range(nb):
                    c_ref[pl.ds(start + h * (cols // halves), own), j * LANES:(j + 1) * LANES] = ref[
                        d, h, j * own:(j + 1) * own, :
                    ]
    gain_cols = dot_dims(c_ref[...], linv_ref[...], 1, 1)
    gain = jnp.concatenate([e_ref[j, 0:rows, :] for j in range(nb)], axis=1)
    out_ref[...] = cov_ref[...] - dot_dims(gain, gain_cols, 1, 1)


def on_device(covariance, state_mean, obs_values, obs_cells, obs_weights, obs_variance):
    rows, cols = covariance.shape
    n_row, n_col = lax.axis_size("row"), lax.axis_size("col")
    n_z = n_row // 2
    row, col = lax.axis_index("row"), lax.axis_index("col")
    plane = 2 * n_col
    batches, _, obs = obs_cells.shape
    m = batches * obs
    nb = m // LANES
    own = rows // plane
    c_rows = own * nb
    s_rows = nb * (nb + 1) // 2 * LANES // plane
    chunk = s_rows + c_rows
    at = jnp.stack([row, col]).astype(jnp.int32)
    mean = state_mean.reshape(1, rows)

    plane_groups = [[z * plane + i for i in range(plane)] for z in range(n_z)]
    z_groups = [[2 * z + k for z in range(n_z)] for k in range(2)]
    pairs = []
    for idx in range(n_row * n_col):
        r, c = divmod(idx, n_col)
        z, k = divmod(r, 2)
        pairs.append((idx, (2 * c + k) * n_col + z))

    send = call(
        project_kernel,
        shape(plane, chunk, LANES),
        [HBM] * 4,
        [
            pltpu.VMEM((rows, m), jnp.float32),
            pltpu.VMEM((m, m), jnp.float32),
            pltpu.VMEM((rows, cols), jnp.float32),
            pltpu.VMEM((1, rows), jnp.float32),
            pltpu.VMEM(obs_cells.shape, jnp.int32),
            pltpu.VMEM(obs_weights.shape, jnp.float32),
            pltpu.SemaphoreType.DMA((4,)),
        ],
        flops=2 * rows * m * (cols + m),
        name="project",
        limit=60 * 1024 * 1024,
    )(covariance, mean, obs_cells, obs_weights)
    got = lax.all_to_all(send, ("row", "col"), 0, 0, axis_index_groups=plane_groups)
    s_chunk = jnp.sum(got[:, :s_rows], axis=0)
    c_own = jnp.sum(got[:, s_rows:].reshape(2, n_col, c_rows, LANES), axis=1)

    s_send = jnp.broadcast_to(s_chunk[None], (n_z, s_rows, LANES))
    def partner(x, bit):
        return lax.ppermute(x, "row", [(i, i ^ bit) for i in range(n_row)])

    def doubled(x, theirs):
        return jnp.concatenate([x[:, None], theirs[:, None]], axis=1).reshape((-1,) + c_own.shape)

    bits = []
    while 1 << len(bits) < n_z:
        bits.append(2 << len(bits))
    pieces = lax.ppermute(c_own, ("row", "col"), pairs)[None]
    theirs = partner(pieces, bits[-1])
    s_all = lax.all_to_all(s_send, "row", 0, 0, axis_index_groups=z_groups)
    s_all, pieces, theirs = lax.optimization_barrier((s_all, pieces, theirs))
    pieces = doubled(pieces, theirs)
    s_full = jnp.sum(s_all, axis=0)
    send2 = jnp.concatenate(
        [
            jnp.broadcast_to(s_full[None], (plane, s_rows, LANES)),
            jnp.broadcast_to(c_own[:, None], (2, n_col, c_rows, LANES)).reshape(plane, c_rows, LANES),
        ],
        axis=1,
    )
    got2 = lax.all_to_all(send2, ("row", "col"), 0, 0, axis_index_groups=plane_groups)

    for bit in bits[-2:0:-1]:
        pieces = doubled(pieces, partner(pieces, bit))
    got2, pieces = lax.optimization_barrier((got2, pieces))
    state = (
        shape(m, m),
        shape(nb, nb, LANES, LANES),
        shape(nb, nb, LANES, LANES),
        shape(nb, rows + SUB, LANES),
        shape(LANES, m),
    )
    theirs = partner(pieces, bits[0])
    held = call(early_kernel, state, [VMEM] * 3, flops=1 << 30, name="early")(
        got2, obs_values.reshape(nb, LANES), obs_variance.reshape(nb, LANES)
    )
    held, theirs = lax.optimization_barrier((held, theirs))
    pieces = doubled(pieces, theirs)
    other = partner(pieces, 1)
    out = call(
        late_kernel,
        state + (shape(1, rows),),
        [VMEM] * 6,
        flops=1 << 30,
        name="late",
        aliases={n + 1: n for n in range(len(state))},
    )(mean, *held)
    linv, e, after = out[0], out[3], out[5]
    updated = call(
        update_kernel,
        shape(rows, cols),
        [VMEM] * 5,
        [pltpu.VMEM((cols, m), jnp.float32)],
        flops=1 << 31,
        name="update",
    )(covariance, pieces, other, linv, e)
    return (updated, after.reshape(rows))


def solution(mesh):
    return jax.shard_map(
        on_device,
        mesh=mesh,
        in_specs=(P("row", "col"), P("row"), P(), P(), P(), P()),
        out_specs=(P("row", "col"), P("row")),
        check_vma=False,
    )
```

```python
import jax
import jax.numpy as jnp
from jax import lax
from jax.experimental import pallas as pl
from jax.experimental.pallas import tpu as pltpu
from jax.sharding import PartitionSpec as P

SUB = 8
LANES = 128
GROUPS = LANES // SUB
HI = lax.Precision.HIGHEST
HBM = pl.BlockSpec(memory_space=pltpu.HBM)
VMEM = pl.BlockSpec(memory_space=pltpu.VMEM)
LIMIT = 48 * 1024 * 1024


def dot(a, b):
    return jnp.dot(a, b, precision=HI, preferred_element_type=jnp.float32)


def dot_dims(a, b, da, db):
    return lax.dot_general(
        a, b, (((da,), (db,)), ((), ())), precision=HI, preferred_element_type=jnp.float32
    )


def wide(x):
    return jnp.broadcast_to(x, (SUB, LANES))


def lower_blocks(n):
    return [(i, j) for i in range(n) for j in range(i + 1)]


def call(kernel, out_shape, specs, scratch=(), flops=0, name=None, aliases=None, limit=LIMIT):
    return pl.pallas_call(
        kernel,
        out_shape=out_shape,
        in_specs=specs,
        out_specs=jax.tree.map(lambda _: VMEM, out_shape),
        scratch_shapes=list(scratch),
        input_output_aliases=aliases or {},
        compiler_params=pltpu.CompilerParams(vmem_limit_bytes=limit),
        cost_estimate=pl.CostEstimate(flops=flops, bytes_accessed=1 << 20, transcendentals=0),
        name=name,
    )


def shape(*dims):
    return jax.ShapeDtypeStruct(dims, jnp.float32)


def operator(cells_ref, weights_ref, batch, start, count):
    foot, obs = cells_ref.shape[1], cells_ref.shape[2]
    positions = start + lax.broadcasted_iota(jnp.int32, (count, obs), 0)
    total = jnp.zeros((count, obs), jnp.float32)
    for f in range(foot):
        hit = cells_ref[batch, f:f + 1, :] == positions
        total = total + jnp.where(hit, weights_ref[batch, f:f + 1, :], 0.0)
    return total


def project_kernel(
    cov_in, mean_in, cells_in, weights_in, send_ref, c_ref, s_ref, cov_ref, mean_ref, cells_ref, weights_ref, sems
):
    moves = [
        pltpu.make_async_copy(src, dst, sems.at[n])
        for n, (src, dst) in enumerate(
            [(cells_in, cells_ref), (weights_in, weights_ref), (cov_in, cov_ref), (mean_in, mean_ref)]
        )
    ]
    for move in moves:
        move.start()
    moves[0].wait()
    moves[1].wait()
    rows, cols = cov_ref.shape
    row, col = lax.axis_index("row"), lax.axis_index("col")
    batches, _, obs = cells_ref.shape
    plane = send_ref.shape[0]
    nb = batches * obs // LANES
    per = obs // LANES
    row_ops = [operator(cells_ref, weights_ref, b, row * rows, rows) for b in range(batches)]
    col_ops = [operator(cells_ref, weights_ref, b, col * cols, cols) for b in range(batches)]
    moves[2].wait()
    moves[3].wait()
    cov = cov_ref[...]
    for b in range(batches):
        c_ref[:, b * obs:(b + 1) * obs] = dot(cov, col_ops[b])
    for i in range(batches):
        for j in range(i + 1):
            s_ref[i * obs:(i + 1) * obs, j * obs:(j + 1) * obs] = dot_dims(
                row_ops[i], c_ref[:, j * obs:(j + 1) * obs], 0, 0
            )
    low = lower_blocks(nb)
    tiles = len(low) * GROUPS // plane
    lane = lax.broadcasted_iota(jnp.int32, (SUB, LANES), 1)
    sub = lax.broadcasted_iota(jnp.int32, (SUB, LANES), 0)
    mean = jnp.broadcast_to(mean_ref[...], (SUB, rows))
    mean = jnp.where(col == 0, mean, 0.0)
    preds = [dot(mean, row_ops[b]) for b in range(batches)]
    for n, (i, j) in enumerate(low):
        for g in range(GROUPS):
            t = s_ref[i * LANES + g * SUB:i * LANES + (g + 1) * SUB, j * LANES:(j + 1) * LANES]
            if i == j and g == 0:
                p = preds[i // per][:, (i % per) * LANES:(i % per + 1) * LANES]
                t = jnp.where((sub == 0) & (lane > 0), p, t)
                t = jnp.where((sub == 1) & (lane == LANES - 1), wide(p[:, :1]), t)
            q = n * GROUPS + g
            send_ref[q // tiles, (q % tiles) * SUB:(q % tiles + 1) * SUB, :] = t
    own = rows // plane
    for i in range(plane):
        for j in range(nb):
            at = (tiles + j) * SUB
            send_ref[i, at:at + own, :] = c_ref[i * own:(i + 1) * own, j * LANES:(j + 1) * LANES]


def inverse_factor(v, jobs):
    v = list(v)
    lane = lax.broadcasted_iota(jnp.int32, (SUB, LANES), 1)
    sub = lax.broadcasted_iota(jnp.int32, (SUB, LANES), 0)
    out = []
    following = None
    for p in range(len(v)):
        last = p + 1 == len(v)
        t = v[p]
        base = p * SUB
        inside = (lane >= base) & (lane < base + SUB)
        col = following or [wide(t[:, base + s:base + s + 1]) for s in range(SUB)]
        ahead, square = [], []
        if not last:
            nxt = base + SUB
            ahead = [wide(t[:, nxt + s:nxt + s + 1]) for s in range(SUB)]
            square = [wide(v[p + 1][:, nxt + s:nxt + s + 1]) for s in range(SUB)]
        t = jnp.where(inside, jnp.where(lane - base == sub, 1.0, 0.0), t)
        low = t
        piv = jnp.ones((SUB, LANES), jnp.float32)
        pairs = []
        for u in range(0, SUB, 2):
            a = wide(col[u][u:u + 1])
            b = wide(col[u + 1][u:u + 1])
            c = wide(col[u + 1][u + 1:u + 2])
            det = a * c - b * b
            rd = pltpu.reciprocal(det, approx=True)
            ra = pltpu.reciprocal(a, approx=True)
            here = (sub == u) | (sub == u + 1)
            c1 = jnp.where(here, 0.0, col[u])
            c2 = jnp.where(here, 0.0, col[u + 1])
            m1 = (c1 * c - c2 * b) * rd
            m2 = (c2 * a - c1 * b) * rd

            def clear(z):
                return z - (m1 * wide(z[u:u + 1]) + m2 * wide(z[u + 1:u + 2]))

            for w in range(u + 2, SUB):
                col[w] = clear(col[w])
            ahead = [clear(z) for z in ahead]
            t = clear(t)
            low = jnp.where(
                sub > u + 1, clear(low), jnp.where(sub == u + 1, low - (b * ra) * wide(low[u:u + 1]), low)
            )
            piv = jnp.where(sub == u, a, jnp.where(sub == u + 1, det * ra, piv))
            pairs.append((a * rd, b * rd, c * rd))
        out.append(jnp.where(lane <= sub + base, low * lax.rsqrt(piv), 0.0))

        def solved(z):
            q = []
            for u in range(0, SUB, 2):
                ar, br, cr = pairs[u // 2]
                z0, z1 = wide(z[u:u + 1]), wide(z[u + 1:u + 2])
                q.extend((z0 * cr - z1 * br, z1 * ar - z0 * br))
            return q

        def less(w, c, q):
            g = [c[s] * q[s] for s in range(SUB)]
            return w - (((g[0] + g[1]) + (g[2] + g[3])) + ((g[4] + g[5]) + (g[6] + g[7])))

        if not last:
            q = solved(t)
            following = None
            for j in range(p + 1, len(v)):
                c = [wide(v[j][:, base + s:base + s + 1]) for s in range(SUB)]
                v[j] = less(jnp.where(inside, 0.0, v[j]), c, q)
                if following is None:
                    following = [less(square[s], c, solved(ahead[s])) for s in range(SUB)]
        if jobs:
            jobs.pop(0)()
    while jobs:
        jobs.pop(0)()
    return jnp.concatenate(out, axis=0)


def prepare(got_ref, values_ref, variance_ref, linv_ref, a_ref, e_ref):
    nb = values_ref.shape[0]
    rows = e_ref.shape[1] - SUB
    low = lower_blocks(nb)
    plane = got_ref.shape[0]
    tiles = len(low) * GROUPS // plane
    own = rows // plane
    for n, (i, j) in enumerate(low):
        for g in range(GROUPS):
            q = n * GROUPS + g
            a_ref[i, j, g * SUB:(g + 1) * SUB, :] = got_ref[
                q // tiles, (q % tiles) * SUB:(q % tiles + 1) * SUB, :
            ]
    for i in range(plane):
        for j in range(nb):
            at = tiles * SUB + j * own
            e_ref[j, i * own:(i + 1) * own, :] = got_ref[i, at:at + own, :]
    r_io = lax.broadcasted_iota(jnp.int32, (LANES, LANES), 0)
    l_io = lax.broadcasted_iota(jnp.int32, (LANES, LANES), 1)
    lane = lax.broadcasted_iota(jnp.int32, (SUB, LANES), 1)
    for i in range(nb):
        first = a_ref[i, i, 0:SUB, :]
        pred = jnp.where(lane == 0, wide(first[1:2, LANES - 1:LANES]), wide(first[0:1, :]))
        e_ref[i, rows:rows + SUB, :] = wide(values_ref[i:i + 1, :]) - pred
        d = a_ref[i, i]
        below = jnp.where(r_io > l_io, d, 0.0)
        diag = jnp.where(r_io == l_io, d + variance_ref[i:i + 1, :], 0.0)
        a_ref[i, i] = below + below.T + diag
    for i in range(nb):
        for j in range(i + 1, nb):
            linv_ref[i * LANES:(i + 1) * LANES, j * LANES:(j + 1) * LANES] = jnp.zeros(
                (LANES, LANES), jnp.float32
            )


def factor_steps(begin, end, linv_ref, a_ref, l_ref, e_ref, y_ref):
    nb = a_ref.shape[0]

    def span(i):
        return slice(i * LANES, (i + 1) * LANES)

    def scale(j, i):
        l_ref[j, i] = dot_dims(a_ref[j, i], linv_ref[span(i), span(i)], 1, 1)

    def reduce(j, k, i):
        a_ref[j, k] = a_ref[j, k] - dot_dims(l_ref[j, i], l_ref[k, i], 1, 1)

    def scale_rows(i):
        e_ref[i] = dot_dims(e_ref[i], linv_ref[span(i), span(i)], 1, 1)

    def reduce_rows(k, i):
        e_ref[k] = e_ref[k] - dot_dims(e_ref[i], l_ref[k, i], 1, 1)

    def gather(i):
        acc = dot(l_ref[i, 0], linv_ref[0:LANES, 0:i * LANES])
        for k in range(1, i):
            acc = acc + dot(l_ref[i, k], linv_ref[span(k), 0:i * LANES])
        y_ref[:, 0:i * LANES] = acc

    def finish(i):
        linv_ref[span(i), 0:i * LANES] = -dot(linv_ref[span(i), span(i)], y_ref[:, 0:i * LANES])

    def work(f, *args):
        return lambda: f(*args)

    def rest(i):
        todo = [work(scale, j, i) for j in range(i + 2, nb)]
        todo += [work(reduce, j, k, i) for k in range(i + 1, nb) for j in range(max(k, i + 2), nb)]
        todo.append(work(scale_rows, i))
        todo += [work(reduce_rows, k, i) for k in range(i + 1, nb)]
        if i > 0:
            todo.append(work(finish, i))
        todo.append(work(gather, i + 1))
        return todo

    for i in range(begin, end):
        jobs = rest(i - 1) if i > 0 else []
        linv_ref[span(i), span(i)] = inverse_factor(
            [a_ref[i, i, g * SUB:(g + 1) * SUB, :] for g in range(GROUPS)], jobs
        )
        if i + 1 < nb:
            scale(i + 1, i)
            reduce(i + 1, i + 1, i)
        else:
            scale_rows(i)
            finish(i)


def early_kernel(got_ref, values_ref, variance_ref, linv_ref, a_ref, l_ref, e_ref, y_ref):
    prepare(got_ref, values_ref, variance_ref, linv_ref, a_ref, e_ref)
    factor_steps(0, a_ref.shape[0] - 2, linv_ref, a_ref, l_ref, e_ref, y_ref)


def middle_kernel(linv_in, a_in, l_in, e_in, y_in, linv_ref, a_ref, l_ref, e_ref, y_ref):
    nb = a_ref.shape[0]
    factor_steps(nb - 2, nb - 1, linv_ref, a_ref, l_ref, e_ref, y_ref)


def late_kernel(
    mean_ref, linv_in, a_in, l_in, e_in, y_in, linv_ref, a_ref, l_ref, e_ref, y_ref, after_ref
):
    nb = a_ref.shape[0]
    rows = e_ref.shape[1] - SUB
    factor_steps(nb - 1, nb, linv_ref, a_ref, l_ref, e_ref, y_ref)
    after = jnp.broadcast_to(mean_ref[...], (SUB, rows))
    for i in range(nb):
        after = after + dot_dims(e_ref[i, rows:rows + SUB, :], e_ref[i, 0:rows, :], 1, 1)
    after_ref[...] = after[0:1]


def update_kernel(cov_ref, mine_ref, other_ref, linv_ref, e_ref, out_ref, c_ref):
    n_z, halves, tall, _ = mine_ref.shape
    rows, cols = cov_ref.shape
    m = c_ref.shape[1]
    nb = m // LANES
    own = tall // nb
    row = lax.axis_index("row")
    core = lax.rem(row, 2)
    z_here = lax.div(row, 2)
    for ref, k in ((mine_ref, core), (other_ref, 1 - core)):
        for d in range(n_z):
            start = pl.multiple_of((k * n_z + lax.bitwise_xor(z_here, d)) * own, own)
            for h in range(halves):
                for j in range(nb):
                    c_ref[pl.ds(start + h * (cols // halves), own), j * LANES:(j + 1) * LANES] = ref[
                        d, h, j * own:(j + 1) * own, :
                    ]
    gain_cols = dot_dims(c_ref[...], linv_ref[...], 1, 1)
    gain = jnp.concatenate([e_ref[j, 0:rows, :] for j in range(nb)], axis=1)
    out_ref[...] = cov_ref[...] - dot_dims(gain, gain_cols, 1, 1)


def on_device(covariance, state_mean, obs_values, obs_cells, obs_weights, obs_variance):
    rows, cols = covariance.shape
    n_row, n_col = lax.axis_size("row"), lax.axis_size("col")
    n_z = n_row // 2
    row, col = lax.axis_index("row"), lax.axis_index("col")
    plane = 2 * n_col
    batches, _, obs = obs_cells.shape
    m = batches * obs
    nb = m // LANES
    own = rows // plane
    c_rows = own * nb
    s_rows = nb * (nb + 1) // 2 * LANES // plane
    chunk = s_rows + c_rows
    at = jnp.stack([row, col]).astype(jnp.int32)
    mean = state_mean.reshape(1, rows)

    plane_groups = [[z * plane + i for i in range(plane)] for z in range(n_z)]
    z_groups = [[2 * z + k for z in range(n_z)] for k in range(2)]
    pairs = []
    for idx in range(n_row * n_col):
        r, c = divmod(idx, n_col)
        z, k = divmod(r, 2)
        pairs.append((idx, (2 * c + k) * n_col + z))

    send = call(
        project_kernel,
        shape(plane, chunk, LANES),
        [HBM] * 4,
        [
            pltpu.VMEM((rows, m), jnp.float32),
            pltpu.VMEM((m, m), jnp.float32),
            pltpu.VMEM((rows, cols), jnp.float32),
            pltpu.VMEM((1, rows), jnp.float32),
            pltpu.VMEM(obs_cells.shape, jnp.int32),
            pltpu.VMEM(obs_weights.shape, jnp.float32),
            pltpu.SemaphoreType.DMA((4,)),
        ],
        flops=2 * rows * m * (cols + m),
        name="project",
        limit=60 * 1024 * 1024,
    )(covariance, mean, obs_cells, obs_weights)
    got = lax.all_to_all(send, ("row", "col"), 0, 0, axis_index_groups=plane_groups)
    s_chunk = jnp.sum(got[:, :s_rows], axis=0)
    c_own = jnp.sum(got[:, s_rows:].reshape(2, n_col, c_rows, LANES), axis=1)

    s_send = jnp.broadcast_to(s_chunk[None], (n_z, s_rows, LANES))
    s_all = lax.all_to_all(s_send, "row", 0, 0, axis_index_groups=z_groups)
    c_tr = lax.ppermute(c_own, ("row", "col"), pairs)
    send2 = jnp.concatenate(
        [
            jnp.broadcast_to(jnp.sum(s_all, axis=0)[None], (plane, s_rows, LANES)),
            jnp.broadcast_to(c_own[:, None], (2, n_col, c_rows, LANES)).reshape(plane, c_rows, LANES),
        ],
        axis=1,
    )
    send2, c_tr = lax.optimization_barrier((send2, c_tr))
    got2 = lax.all_to_all(send2, ("row", "col"), 0, 0, axis_index_groups=plane_groups)

    def partner(x, bit):
        return lax.ppermute(x, "row", [(i, i ^ bit) for i in range(n_row)])

    def doubled(x, theirs):
        return jnp.concatenate([x[:, None], theirs[:, None]], axis=1).reshape((-1,) + c_tr.shape)

    bits = []
    while 1 << len(bits) < n_z:
        bits.append(2 << len(bits))
    pieces = c_tr[None]
    for bit in bits[:2:-1]:
        pieces = doubled(pieces, partner(pieces, bit))
    got2, pieces = lax.optimization_barrier((got2, pieces))
    state = (
        shape(m, m),
        shape(nb, nb, LANES, LANES),
        shape(nb, nb, LANES, LANES),
        shape(nb, rows + SUB, LANES),
        shape(LANES, m),
    )
    theirs = partner(pieces, bits[2])
    held = call(early_kernel, state, [VMEM] * 3, flops=1 << 30, name="early")(
        got2, obs_values.reshape(nb, LANES), obs_variance.reshape(nb, LANES)
    )
    held, theirs = lax.optimization_barrier((held, theirs))
    pieces = doubled(pieces, theirs)
    theirs = partner(pieces, bits[1])
    held = call(
        middle_kernel,
        state,
        [VMEM] * 5,
        flops=1 << 30,
        name="middle",
        aliases={n: n for n in range(len(state))},
    )(*held)
    held, theirs = lax.optimization_barrier((held, theirs))
    pieces = doubled(pieces, theirs)
    theirs = partner(pieces, bits[0])
    out = call(
        late_kernel,
        state + (shape(1, rows),),
        [VMEM] * 6,
        flops=1 << 30,
        name="late",
        aliases={n + 1: n for n in range(len(state))},
    )(mean, *held)
    out, theirs = lax.optimization_barrier((out, theirs))
    pieces = doubled(pieces, theirs)
    other = partner(pieces, 1)
    linv, e, after = out[0], out[3], out[5]
    updated = call(
        update_kernel,
        shape(rows, cols),
        [VMEM] * 5,
        [pltpu.VMEM((cols, m), jnp.float32)],
        flops=1 << 31,
        name="update",
    )(covariance, pieces, other, linv, e)
    return (updated, after.reshape(rows))


def solution(mesh):
    return jax.shard_map(
        on_device,
        mesh=mesh,
        in_specs=(P("row", "col"), P("row"), P(), P(), P(), P()),
        out_specs=(P("row", "col"), P("row")),
        check_vma=False,
    )
```

```python
import jax
import jax.numpy as jnp
from jax import lax
from jax.experimental import pallas as pl
from jax.experimental.pallas import tpu as pltpu
from jax.sharding import PartitionSpec as P

SUB = 8
LANES = 128
GROUPS = LANES // SUB
HI = lax.Precision.HIGHEST
HBM = pl.BlockSpec(memory_space=pltpu.HBM)
VMEM = pl.BlockSpec(memory_space=pltpu.VMEM)
LIMIT = 48 * 1024 * 1024


def dot(a, b):
    return jnp.dot(a, b, precision=HI, preferred_element_type=jnp.float32)


def dot_dims(a, b, da, db):
    return lax.dot_general(
        a, b, (((da,), (db,)), ((), ())), precision=HI, preferred_element_type=jnp.float32
    )


def wide(x):
    return jnp.broadcast_to(x, (SUB, LANES))


def lower_blocks(n):
    return [(i, j) for i in range(n) for j in range(i + 1)]


def call(kernel, out_shape, specs, scratch=(), flops=0, name=None, aliases=None, limit=LIMIT):
    return pl.pallas_call(
        kernel,
        out_shape=out_shape,
        in_specs=specs,
        out_specs=jax.tree.map(lambda _: VMEM, out_shape),
        scratch_shapes=list(scratch),
        input_output_aliases=aliases or {},
        compiler_params=pltpu.CompilerParams(vmem_limit_bytes=limit),
        cost_estimate=pl.CostEstimate(flops=flops, bytes_accessed=1 << 20, transcendentals=0),
        name=name,
    )


def shape(*dims):
    return jax.ShapeDtypeStruct(dims, jnp.float32)


def operator(cells_ref, weights_ref, batch, start, count):
    foot, obs = cells_ref.shape[1], cells_ref.shape[2]
    positions = start + lax.broadcasted_iota(jnp.int32, (count, obs), 0)
    total = jnp.zeros((count, obs), jnp.float32)
    for f in range(foot):
        hit = cells_ref[batch, f:f + 1, :] == positions
        total = total + jnp.where(hit, weights_ref[batch, f:f + 1, :], 0.0)
    return total


def project_kernel(
    cov_in, mean_in, cells_in, weights_in, send_ref, c_ref, s_ref, cov_ref, mean_ref, cells_ref, weights_ref, sems
):
    moves = [
        pltpu.make_async_copy(src, dst, sems.at[n])
        for n, (src, dst) in enumerate(
            [(cells_in, cells_ref), (weights_in, weights_ref), (cov_in, cov_ref), (mean_in, mean_ref)]
        )
    ]
    for move in moves:
        move.start()
    moves[0].wait()
    moves[1].wait()
    rows, cols = cov_ref.shape
    row, col = lax.axis_index("row"), lax.axis_index("col")
    batches, _, obs = cells_ref.shape
    plane = send_ref.shape[0]
    nb = batches * obs // LANES
    per = obs // LANES
    row_ops = [operator(cells_ref, weights_ref, b, row * rows, rows) for b in range(batches)]
    col_ops = [operator(cells_ref, weights_ref, b, col * cols, cols) for b in range(batches)]
    moves[2].wait()
    moves[3].wait()
    cov = cov_ref[...]
    for b in range(batches):
        c_ref[:, b * obs:(b + 1) * obs] = dot(cov, col_ops[b])
    for i in range(batches):
        for j in range(i + 1):
            s_ref[i * obs:(i + 1) * obs, j * obs:(j + 1) * obs] = dot_dims(
                row_ops[i], c_ref[:, j * obs:(j + 1) * obs], 0, 0
            )
    low = lower_blocks(nb)
    tiles = len(low) * GROUPS // plane
    lane = lax.broadcasted_iota(jnp.int32, (SUB, LANES), 1)
    sub = lax.broadcasted_iota(jnp.int32, (SUB, LANES), 0)
    mean = jnp.broadcast_to(mean_ref[...], (SUB, rows))
    mean = jnp.where(col == 0, mean, 0.0)
    preds = [dot(mean, row_ops[b]) for b in range(batches)]
    for n, (i, j) in enumerate(low):
        for g in range(GROUPS):
            t = s_ref[i * LANES + g * SUB:i * LANES + (g + 1) * SUB, j * LANES:(j + 1) * LANES]
            if i == j and g == 0:
                p = preds[i // per][:, (i % per) * LANES:(i % per + 1) * LANES]
                t = jnp.where((sub == 0) & (lane > 0), p, t)
                t = jnp.where((sub == 1) & (lane == LANES - 1), wide(p[:, :1]), t)
            q = n * GROUPS + g
            send_ref[q // tiles, (q % tiles) * SUB:(q % tiles + 1) * SUB, :] = t
    own = rows // plane
    for i in range(plane):
        for j in range(nb):
            at = (tiles + j) * SUB
            send_ref[i, at:at + own, :] = c_ref[i * own:(i + 1) * own, j * LANES:(j + 1) * LANES]


def inverse_factor(v, jobs):
    v = list(v)
    lane = lax.broadcasted_iota(jnp.int32, (SUB, LANES), 1)
    sub = lax.broadcasted_iota(jnp.int32, (SUB, LANES), 0)
    out = []
    following = None
    for p in range(len(v)):
        last = p + 1 == len(v)
        t = v[p]
        base = p * SUB
        inside = (lane >= base) & (lane < base + SUB)
        col = following or [wide(t[:, base + s:base + s + 1]) for s in range(SUB)]
        ahead, square = [], []
        if not last:
            nxt = base + SUB
            ahead = [wide(t[:, nxt + s:nxt + s + 1]) for s in range(SUB)]
            square = [wide(v[p + 1][:, nxt + s:nxt + s + 1]) for s in range(SUB)]
        t = jnp.where(inside, jnp.where(lane - base == sub, 1.0, 0.0), t)
        low = t
        piv = jnp.ones((SUB, LANES), jnp.float32)
        pairs = []
        for u in range(0, SUB, 2):
            a = wide(col[u][u:u + 1])
            b = wide(col[u + 1][u:u + 1])
            c = wide(col[u + 1][u + 1:u + 2])
            det = a * c - b * b
            rd = pltpu.reciprocal(det, approx=True)
            ra = pltpu.reciprocal(a, approx=True)
            here = (sub == u) | (sub == u + 1)
            c1 = jnp.where(here, 0.0, col[u])
            c2 = jnp.where(here, 0.0, col[u + 1])
            m1 = (c1 * c - c2 * b) * rd
            m2 = (c2 * a - c1 * b) * rd

            def clear(z):
                return z - (m1 * wide(z[u:u + 1]) + m2 * wide(z[u + 1:u + 2]))

            for w in range(u + 2, SUB):
                col[w] = clear(col[w])
            ahead = [clear(z) for z in ahead]
            t = clear(t)
            low = jnp.where(
                sub > u + 1, clear(low), jnp.where(sub == u + 1, low - (b * ra) * wide(low[u:u + 1]), low)
            )
            piv = jnp.where(sub == u, a, jnp.where(sub == u + 1, det * ra, piv))
            pairs.append((a * rd, b * rd, c * rd))
        out.append(jnp.where(lane <= sub + base, low * lax.rsqrt(piv), 0.0))

        def solved(z):
            q = []
            for u in range(0, SUB, 2):
                ar, br, cr = pairs[u // 2]
                z0, z1 = wide(z[u:u + 1]), wide(z[u + 1:u + 2])
                q.extend((z0 * cr - z1 * br, z1 * ar - z0 * br))
            return q

        def less(w, c, q):
            g = [c[s] * q[s] for s in range(SUB)]
            return w - (((g[0] + g[1]) + (g[2] + g[3])) + ((g[4] + g[5]) + (g[6] + g[7])))

        if not last:
            q = solved(t)
            following = None
            for j in range(p + 1, len(v)):
                c = [wide(v[j][:, base + s:base + s + 1]) for s in range(SUB)]
                v[j] = less(jnp.where(inside, 0.0, v[j]), c, q)
                if following is None:
                    following = [less(square[s], c, solved(ahead[s])) for s in range(SUB)]
        if jobs:
            jobs.pop(0)()
    while jobs:
        jobs.pop(0)()
    return jnp.concatenate(out, axis=0)


def prepare(got_ref, values_ref, variance_ref, linv_ref, a_ref, e_ref):
    nb = values_ref.shape[0]
    rows = e_ref.shape[1] - SUB
    low = lower_blocks(nb)
    plane = got_ref.shape[0]
    tiles = len(low) * GROUPS // plane
    own = rows // plane
    for n, (i, j) in enumerate(low):
        for g in range(GROUPS):
            q = n * GROUPS + g
            a_ref[i, j, g * SUB:(g + 1) * SUB, :] = got_ref[
                q // tiles, (q % tiles) * SUB:(q % tiles + 1) * SUB, :
            ]
    for i in range(plane):
        for j in range(nb):
            at = tiles * SUB + j * own
            e_ref[j, i * own:(i + 1) * own, :] = got_ref[i, at:at + own, :]
    r_io = lax.broadcasted_iota(jnp.int32, (LANES, LANES), 0)
    l_io = lax.broadcasted_iota(jnp.int32, (LANES, LANES), 1)
    lane = lax.broadcasted_iota(jnp.int32, (SUB, LANES), 1)
    for i in range(nb):
        first = a_ref[i, i, 0:SUB, :]
        pred = jnp.where(lane == 0, wide(first[1:2, LANES - 1:LANES]), wide(first[0:1, :]))
        e_ref[i, rows:rows + SUB, :] = wide(values_ref[i:i + 1, :]) - pred
        d = a_ref[i, i]
        below = jnp.where(r_io > l_io, d, 0.0)
        diag = jnp.where(r_io == l_io, d + variance_ref[i:i + 1, :], 0.0)
        a_ref[i, i] = below + below.T + diag
    for i in range(nb):
        for j in range(i + 1, nb):
            linv_ref[i * LANES:(i + 1) * LANES, j * LANES:(j + 1) * LANES] = jnp.zeros(
                (LANES, LANES), jnp.float32
            )


def factor_steps(begin, end, linv_ref, a_ref, l_ref, e_ref, y_ref):
    nb = a_ref.shape[0]

    def span(i):
        return slice(i * LANES, (i + 1) * LANES)

    def scale(j, i):
        l_ref[j, i] = dot_dims(a_ref[j, i], linv_ref[span(i), span(i)], 1, 1)

    def reduce(j, k, i):
        a_ref[j, k] = a_ref[j, k] - dot_dims(l_ref[j, i], l_ref[k, i], 1, 1)

    def scale_rows(i):
        e_ref[i] = dot_dims(e_ref[i], linv_ref[span(i), span(i)], 1, 1)

    def reduce_rows(k, i):
        e_ref[k] = e_ref[k] - dot_dims(e_ref[i], l_ref[k, i], 1, 1)

    def gather(i):
        acc = dot(l_ref[i, 0], linv_ref[0:LANES, 0:i * LANES])
        for k in range(1, i):
            acc = acc + dot(l_ref[i, k], linv_ref[span(k), 0:i * LANES])
        y_ref[:, 0:i * LANES] = acc

    def finish(i):
        linv_ref[span(i), 0:i * LANES] = -dot(linv_ref[span(i), span(i)], y_ref[:, 0:i * LANES])

    def work(f, *args):
        return lambda: f(*args)

    def rest(i):
        todo = [work(scale, j, i) for j in range(i + 2, nb)]
        todo += [work(reduce, j, k, i) for k in range(i + 1, nb) for j in range(max(k, i + 2), nb)]
        todo.append(work(scale_rows, i))
        todo += [work(reduce_rows, k, i) for k in range(i + 1, nb)]
        if i > 0:
            todo.append(work(finish, i))
        todo.append(work(gather, i + 1))
        return todo

    for i in range(begin, end):
        jobs = rest(i - 1) if i > 0 else []
        linv_ref[span(i), span(i)] = inverse_factor(
            [a_ref[i, i, g * SUB:(g + 1) * SUB, :] for g in range(GROUPS)], jobs
        )
        if i + 1 < nb:
            scale(i + 1, i)
            reduce(i + 1, i + 1, i)
        else:
            scale_rows(i)
            finish(i)


def early_kernel(got_ref, values_ref, variance_ref, linv_ref, a_ref, l_ref, e_ref, y_ref):
    prepare(got_ref, values_ref, variance_ref, linv_ref, a_ref, e_ref)
    factor_steps(0, a_ref.shape[0] - 2, linv_ref, a_ref, l_ref, e_ref, y_ref)


def middle_kernel(linv_in, a_in, l_in, e_in, y_in, linv_ref, a_ref, l_ref, e_ref, y_ref):
    nb = a_ref.shape[0]
    factor_steps(nb - 2, nb - 1, linv_ref, a_ref, l_ref, e_ref, y_ref)


def late_kernel(
    mean_ref, linv_in, a_in, l_in, e_in, y_in, linv_ref, a_ref, l_ref, e_ref, y_ref, after_ref
):
    nb = a_ref.shape[0]
    rows = e_ref.shape[1] - SUB
    factor_steps(nb - 1, nb, linv_ref, a_ref, l_ref, e_ref, y_ref)
    after = jnp.broadcast_to(mean_ref[...], (SUB, rows))
    for i in range(nb):
        after = after + dot_dims(e_ref[i, rows:rows + SUB, :], e_ref[i, 0:rows, :], 1, 1)
    after_ref[...] = after[0:1]


def half_kernel(pieces_ref, linv_ref, out_ref, c_ref):
    n_z, halves, tall, _ = pieces_ref.shape
    nb = c_ref.shape[1] // LANES
    own = tall // nb
    here = lax.div(lax.axis_index("row"), 2)
    for d in range(n_z):
        start = pl.multiple_of(lax.bitwise_xor(here, d) * own, own)
        for h in range(halves):
            for j in range(nb):
                c_ref[pl.ds(start + h * n_z * own, own), j * LANES:(j + 1) * LANES] = pieces_ref[
                    d, h, j * own:(j + 1) * own, :
                ]
    out_ref[...] = dot_dims(c_ref[...], linv_ref[...], 1, 1)


def update_kernel(cov_ref, mine_ref, other_ref, linv_ref, e_ref, out_ref, c_ref, t_ref, g_ref):
    rows, m = cov_ref.shape[0], c_ref.shape[1]
    halves = other_ref.shape[1]
    part = c_ref.shape[0] // halves
    core = lax.rem(lax.axis_index("row"), 2)
    half_kernel(other_ref, linv_ref, t_ref, c_ref)
    for h in range(halves):
        for k, ref in ((core, mine_ref), (1 - core, t_ref)):
            start = pl.multiple_of((2 * h + k) * part, part)
            g_ref[pl.ds(start, part), :] = ref[h * part:(h + 1) * part, :]
    gain = jnp.concatenate([e_ref[j, 0:rows, :] for j in range(m // LANES)], axis=1)
    out_ref[...] = cov_ref[...] - dot_dims(gain, g_ref[...], 1, 1)


def on_device(covariance, state_mean, obs_values, obs_cells, obs_weights, obs_variance):
    rows, cols = covariance.shape
    n_row, n_col = lax.axis_size("row"), lax.axis_size("col")
    n_z = n_row // 2
    row, col = lax.axis_index("row"), lax.axis_index("col")
    plane = 2 * n_col
    batches, _, obs = obs_cells.shape
    m = batches * obs
    nb = m // LANES
    own = rows // plane
    c_rows = own * nb
    s_rows = nb * (nb + 1) // 2 * LANES // plane
    chunk = s_rows + c_rows
    at = jnp.stack([row, col]).astype(jnp.int32)
    mean = state_mean.reshape(1, rows)

    plane_groups = [[z * plane + i for i in range(plane)] for z in range(n_z)]
    z_groups = [[2 * z + k for z in range(n_z)] for k in range(2)]
    pairs = []
    for idx in range(n_row * n_col):
        r, c = divmod(idx, n_col)
        z, k = divmod(r, 2)
        pairs.append((idx, (2 * c + k) * n_col + z))

    send = call(
        project_kernel,
        shape(plane, chunk, LANES),
        [HBM] * 4,
        [
            pltpu.VMEM((rows, m), jnp.float32),
            pltpu.VMEM((m, m), jnp.float32),
            pltpu.VMEM((rows, cols), jnp.float32),
            pltpu.VMEM((1, rows), jnp.float32),
            pltpu.VMEM(obs_cells.shape, jnp.int32),
            pltpu.VMEM(obs_weights.shape, jnp.float32),
            pltpu.SemaphoreType.DMA((4,)),
        ],
        flops=2 * rows * m * (cols + m),
        name="project",
        limit=60 * 1024 * 1024,
    )(covariance, mean, obs_cells, obs_weights)
    got = lax.all_to_all(send, ("row", "col"), 0, 0, axis_index_groups=plane_groups)
    s_chunk = jnp.sum(got[:, :s_rows], axis=0)
    c_own = jnp.sum(got[:, s_rows:].reshape(2, n_col, c_rows, LANES), axis=1)

    s_send = jnp.broadcast_to(s_chunk[None], (n_z, s_rows, LANES))
    s_all = lax.all_to_all(s_send, "row", 0, 0, axis_index_groups=z_groups)
    c_tr = lax.ppermute(c_own, ("row", "col"), pairs)
    send2 = jnp.concatenate(
        [
            jnp.broadcast_to(jnp.sum(s_all, axis=0)[None], (plane, s_rows, LANES)),
            jnp.broadcast_to(c_own[:, None], (2, n_col, c_rows, LANES)).reshape(plane, c_rows, LANES),
        ],
        axis=1,
    )
    send2, c_tr = lax.optimization_barrier((send2, c_tr))
    got2 = lax.all_to_all(send2, ("row", "col"), 0, 0, axis_index_groups=plane_groups)

    def partner(x, bit):
        return lax.ppermute(x, "row", [(i, i ^ bit) for i in range(n_row)])

    def doubled(x, theirs):
        return jnp.concatenate([x[:, None], theirs[:, None]], axis=1).reshape((-1,) + c_tr.shape)

    bits = []
    while 1 << len(bits) < n_z:
        bits.append(2 << len(bits))
    pieces = c_tr[None]
    for bit in bits[:2:-1]:
        pieces = doubled(pieces, partner(pieces, bit))
    got2, pieces = lax.optimization_barrier((got2, pieces))
    state = (
        shape(m, m),
        shape(nb, nb, LANES, LANES),
        shape(nb, nb, LANES, LANES),
        shape(nb, rows + SUB, LANES),
        shape(LANES, m),
    )
    theirs = partner(pieces, bits[2])
    held = call(early_kernel, state, [VMEM] * 3, flops=1 << 30, name="early")(
        got2, obs_values.reshape(nb, LANES), obs_variance.reshape(nb, LANES)
    )
    held, theirs = lax.optimization_barrier((held, theirs))
    pieces = doubled(pieces, theirs)
    theirs = partner(pieces, bits[1])
    held = call(
        middle_kernel,
        state,
        [VMEM] * 5,
        flops=1 << 30,
        name="middle",
        aliases={n: n for n in range(len(state))},
    )(*held)
    held, theirs = lax.optimization_barrier((held, theirs))
    pieces = doubled(pieces, theirs)
    theirs = partner(pieces, bits[0])
    out = call(
        late_kernel,
        state + (shape(1, rows),),
        [VMEM] * 6,
        flops=1 << 30,
        name="late",
        aliases={n + 1: n for n in range(len(state))},
    )(mean, *held)
    out, theirs = lax.optimization_barrier((out, theirs))
    pieces = doubled(pieces, theirs)
    other = partner(pieces, 1)
    linv, e, after = out[0], out[3], out[5]
    half = (cols // 2, m)
    mine = call(
        half_kernel,
        shape(*half),
        [VMEM] * 2,
        [pltpu.VMEM(half, jnp.float32)],
        flops=1 << 30,
        name="half",
    )(pieces, linv)
    updated = call(
        update_kernel,
        shape(rows, cols),
        [VMEM] * 5,
        [pltpu.VMEM(half, jnp.float32), pltpu.VMEM(half, jnp.float32), pltpu.VMEM((cols, m), jnp.float32)],
        flops=1 << 31,
        name="update",
    )(covariance, mine, other, linv, e)
    return (updated, after.reshape(rows))


def solution(mesh):
    return jax.shard_map(
        on_device,
        mesh=mesh,
        in_specs=(P("row", "col"), P("row"), P(), P(), P(), P()),
        out_specs=(P("row", "col"), P("row")),
        check_vma=False,
    )
```
